128 devices in a mesh: pair: 8 (over z_hi, y), blk: 16 (over z_lo, x, core).
Axes of the slice: x: 4, y: 4, z: 4 (z_hi: 2, z_lo: 2; z = z_hi * 2 + z_lo), core: 2. Of those that a mesh axis runs over, the one named last changes fastest.
Arguments:
- source: bfloat16 [32768, 1024], P(('pair', 'blk'))
- source_label: int32 [32768], P(('pair', 'blk')), may hold values from 0 to 7, as said below
- target: bfloat16 [32768, 1024], P(('pair', 'blk'))
- target_label: int32 [32768], P(('pair', 'blk')), may hold values from 0 to 7, as said below
Outputs:
- src_partner: float32 [32768, 1024], P(('pair', 'blk'))
- src_margin: float32 [32768], P(('pair', 'blk'))
- tgt_margin: float32 [32768], P(('pair', 'blk'))
The draws below stay inside these ranges and needn't reach their ends.
Inputs may be any that keep to these rules, and one draw needn't show every extreme that they name: `source_label`: rows (i * 16 + k) * 256 to (i * 16 + k + 1) * 256 - 1 form block (i, k). For every k below 8, blocks (i, k) and (i, k + 8) together name every bucket exactly 64 times, so a block names one bucket at most 64 times, and in every draw some block names one bucket 64 times. `target_label`: rows (i * 16 + k) * 256 to (i * 16 + k + 1) * 256 - 1 form block (i, k). For every k below 8, blocks (i, k) and (i, k + 8) together name every bucket exactly 64 times, so a block names one bucket at most 64 times, and in every draw some block names one bucket 64 times.
All inputs are finite; a program needn't handle non-finite values.
Results may differ from the reference program's by a relative error of at most 0.0041.
Values may be sent and summed in bfloat16 or wider, within the bound.
No kernel may reach another device: no remote copies, remote signals or barrier semaphores. Data moves between devices by JAX's collectives and lax.ppermute only.
A program may use at most 128 MiB of HBM per device.

```python
from functools import partial
import jax
import jax.numpy as jnp
from jax import lax

D = 1024
ROWS = 256
BUCKETS = 8
COLUMNS = 16
CAP = 64
GROUP = 4096
ROWS_ALL = 32768


clusters = 32


def shared_parts(seed_key):
    key_center, key_column = jax.random.split(seed_key, 2)
    centers = jax.random.normal(key_center, (clusters, D), jnp.float32)
    column_scale = jnp.exp(jax.random.uniform(key_column, (D,), jnp.float32, jnp.log(0.3), jnp.log(3.0)))
    return (centers, column_scale)


def sentence_rows(seed_key, centers, column_scale, scale_low, scale_high):
    key_pick = jax.random.fold_in(seed_key, 0)
    key_weight = jax.random.fold_in(seed_key, 1)
    key_gauss = jax.random.fold_in(seed_key, 2)
    key_scale = jax.random.fold_in(seed_key, 4)
    cluster_pick = jax.random.randint(key_pick, (ROWS_ALL,), 0, clusters)
    strength = jax.random.uniform(key_weight, (ROWS_ALL, 1), jnp.float32, 0.5, 2.0)
    gauss_noise = jax.random.normal(key_gauss, (ROWS_ALL, D), jnp.float32)
    mixed_noise = gauss_noise
    row_scale = jnp.exp(jax.random.uniform(key_scale, (ROWS_ALL, 1), jnp.float32, jnp.log(scale_low), jnp.log(scale_high)))
    values = (mixed_noise + strength * centers[cluster_pick]) * column_scale[None, :] * row_scale
    return values.astype(jnp.bfloat16)


def bucket_labels(seed_key):
    key_column, key_hot, key_rows, key_mix = jax.random.split(seed_key, 4)
    half_cols = COLUMNS // 2
    col_star = jax.random.randint(key_column, (), 0, half_cols)
    hot_star = jax.random.randint(key_hot, (), 0, BUCKETS)
    slot_bucket = jnp.arange(2 * ROWS, dtype=jnp.int32) // CAP

    def one_pair(pair_index):
        column = pair_index % half_cols
        slot_order = jax.random.permutation(jax.random.fold_in(key_rows, pair_index), 2 * ROWS).astype(jnp.int32)
        slot_rank = jnp.zeros((2 * ROWS,), jnp.int32).at[slot_order].set(jnp.arange(2 * ROWS, dtype=jnp.int32))
        forced = (column == col_star) & (slot_bucket == hot_star)
        slot_score = jnp.where(forced, 0, slot_rank + 1)
        picked = jnp.argsort(slot_score, stable=True)
        kept_labels = slot_bucket[picked[:ROWS]]
        rest_labels = slot_bucket[picked[ROWS:]]
        key_first, key_second = jax.random.split(jax.random.fold_in(key_mix, pair_index))
        kept_labels = kept_labels[jax.random.permutation(key_first, ROWS)]
        rest_labels = rest_labels[jax.random.permutation(key_second, ROWS)]
        return (kept_labels, rest_labels)
    kept_labels, rest_labels = jax.vmap(one_pair)(jnp.arange(BUCKETS * half_cols, dtype=jnp.int32))
    kept_labels = kept_labels.reshape(BUCKETS, half_cols, ROWS)
    rest_labels = rest_labels.reshape(BUCKETS, half_cols, ROWS)
    return jnp.concatenate([kept_labels, rest_labels], axis=1).reshape(ROWS_ALL).astype(jnp.int32)


def draw_source(key, part):
    centers, column_scale = shared_parts(key)
    key = jax.random.fold_in(key, 11)
    return sentence_rows(key, centers, column_scale, 1.0, 10.0)


def draw_target(key, part):
    centers, column_scale = shared_parts(key)
    key = jax.random.fold_in(key, 12)
    return sentence_rows(key, centers, column_scale, 1.0, 10.0)


def draw_source_label(key, part):
    key = jax.random.fold_in(key, 21)
    return bucket_labels(key)


def draw_target_label(key, part):
    key = jax.random.fold_in(key, 22)
    return bucket_labels(key)


def setup_inputs(seed: int = 0) -> dict:
    splits = jax.random.split(jax.random.key(seed), 5)
    source = draw_source(jax.random.fold_in(splits[4], 71), 0)
    source_label = draw_source_label(jax.random.fold_in(splits[4], 71), 0)
    target = draw_target(jax.random.fold_in(splits[4], 71), 0)
    target_label = draw_target_label(jax.random.fold_in(splits[4], 71), 0)
    return {"source": source, "source_label": source_label, "target": target, "target_label": target_label}


sharpness = 12.0

def normalize(row_block):
    values = row_block.astype(jnp.float32)
    square = lax.optimization_barrier(jnp.mean(values * values, axis=-1, keepdims=True))
    return (values * lax.rsqrt(square + 1e-06)).astype(jnp.bfloat16)

def bucket_scores(orders, src_norm, tgt_norm):
    src_order, tgt_order = orders
    sources = src_norm[src_order]
    targets = tgt_norm[tgt_order]
    similar = lax.dot_general(sources, targets, (((1,), (1,)), ((), ())), preferred_element_type=jnp.float32) / D
    weight = jnp.exp(sharpness * similar)
    fwd_total = lax.optimization_barrier(jnp.sum(weight, axis=1))
    bwd_total = lax.optimization_barrier(jnp.sum(weight, axis=0))
    weighted = weight * similar
    fwd_stat = lax.optimization_barrier(jnp.sum(weighted, axis=1)) / fwd_total
    bwd_stat = lax.optimization_barrier(jnp.sum(weighted, axis=0)) / bwd_total
    partner = jnp.dot(weight.astype(jnp.bfloat16), targets, preferred_element_type=jnp.float32) / fwd_total[:, None]
    back_mean = jnp.dot(weight, bwd_stat, precision=lax.Precision.HIGHEST) / fwd_total
    fore_mean = jnp.dot(fwd_stat, weight, precision=lax.Precision.HIGHEST) / bwd_total
    src_margin = fwd_stat - 0.5 * (fwd_stat + back_mean)
    tgt_margin = bwd_stat - 0.5 * (bwd_stat + fore_mean)
    return (partner, src_margin, tgt_margin)

def reference(source, source_label, target, target_label):
    src_norm = normalize(source)
    tgt_norm = normalize(target)
    src_order = jnp.argsort(source_label, stable=True).astype(jnp.int32).reshape(BUCKETS, GROUP)
    tgt_order = jnp.argsort(target_label, stable=True).astype(jnp.int32).reshape(BUCKETS, GROUP)
    scorer = partial(bucket_scores, src_norm=src_norm, tgt_norm=tgt_norm)
    partner, src_margin, tgt_margin = lax.map(scorer, (src_order, tgt_order))
    flat_src = src_order.reshape(-1)
    flat_tgt = tgt_order.reshape(-1)
    partner_out = jnp.zeros((ROWS_ALL, D), jnp.float32).at[flat_src].set(partner.reshape(-1, D))
    src_out = jnp.zeros((ROWS_ALL,), jnp.float32).at[flat_src].set(src_margin.reshape(-1))
    tgt_out = jnp.zeros((ROWS_ALL,), jnp.float32).at[flat_tgt].set(tgt_margin.reshape(-1))
    return (partner_out, src_out, tgt_out)
```

```python
from functools import partial

import jax
import jax.numpy as jnp
from jax import lax
from jax.experimental import pallas as pl
from jax.experimental.pallas import tpu as pltpu
from jax.sharding import Mesh, PartitionSpec as P

F32, BF16, I32 = jnp.float32, jnp.bfloat16, jnp.int32
SHARP = 12.0
WIDTH = 1024
ROWS = 256
SLOTS = 64
PACK = 512
EXTRA = 128
VMEM_LIMIT = 56 * 2**20
AXES = ("zh", "y", "zl", "x", "c")
ROUTE = ("zh", "y", "zl")
PLANE = ("zl", "x")
RIGHT = [(i, (i + 1) % 4) for i in range(4)]
LEFT = [(i, (i + 3) % 4) for i in range(4)]
SWAP = [(0, 1), (1, 0)]


def params():
    return pltpu.CompilerParams(vmem_limit_bytes=VMEM_LIMIT)


def vm():
    return pl.BlockSpec(memory_space=pltpu.VMEM)


def sm():
    return pl.BlockSpec(memory_space=pltpu.SMEM)


def hbm():
    return pl.BlockSpec(memory_space=pl.ANY)


def route_matrix(labels, half):
    mine = lax.broadcasted_iota(I32, (8, ROWS), 0) == labels
    upper = lax.broadcasted_iota(I32, (ROWS, ROWS), 0) < lax.broadcasted_iota(I32, (ROWS, ROWS), 1)
    before = jnp.dot(mine.astype(BF16), upper.astype(BF16), preferred_element_type=F32)
    rank = jnp.sum(jnp.where(mine, before, 0.0), axis=0, keepdims=True).astype(I32)
    slot = labels * SLOTS + jnp.where(half == 0, rank, SLOTS - 1 - rank)
    return (lax.broadcasted_iota(I32, (PACK, ROWS), 0) == slot).astype(BF16)


def pack_kernel(idx, labels, rows, out):
    values = rows[...].astype(F32)
    square = jnp.mean(values * values, axis=-1, keepdims=True)
    normed = (values * lax.rsqrt(square + 1e-06)).astype(BF16)
    out[...] = jnp.dot(route_matrix(labels[...], idx[0]), normed, preferred_element_type=F32).astype(BF16)


def pack(idx, labels, rows):
    return pl.pallas_call(
        pack_kernel,
        out_shape=jax.ShapeDtypeStruct((PACK, WIDTH), BF16),
        in_specs=[sm(), vm(), vm()],
        out_specs=vm(),
        compiler_params=params(),
        cost_estimate=pl.CostEstimate(flops=2 * PACK * ROWS * WIDTH, bytes_accessed=3 * 2**19, transcendentals=ROWS),
    )(idx, labels, rows)


def score_kernel(sib_first, own, sib, *refs):
    halves = refs[:16]
    weight, fwd, tot, wsum, partner = refs[16:21]
    targets, srcs, weight_bf, acc_t, acc_s, sems = refs[21:]
    for n, half in enumerate(halves):
        pltpu.make_async_copy(half, targets.at[n // 2, pl.ds(128 * (n % 2), 128)], sems.at[n // 2]).start()
    srcs[pl.ds(0, ROWS)] = own[...]
    srcs[pl.ds(ROWS, ROWS)] = sib[...]
    acc_t[...] = jnp.zeros_like(acc_t)
    acc_s[...] = jnp.zeros_like(acc_s)

    def block(n, carry):
        pltpu.make_async_copy(targets.at[n], targets.at[n], sems.at[n]).wait()
        cols_t, cols_s = jnp.zeros((1, ROWS), F32), jnp.zeros((1, ROWS), F32)
        for m in range(2):
            part = pl.ds(ROWS * m, ROWS)
            similar = lax.dot_general(
                srcs[part], targets[n], (((1,), (1,)), ((), ())), preferred_element_type=F32
            ) * (1.0 / WIDTH)
            w = jnp.exp(SHARP * similar)
            weighted = w * similar
            weight[n, part] = w
            weight_bf[n, part] = w.astype(BF16)
            acc_t[part] += w[:, :128] + w[:, 128:]
            acc_s[part] += weighted[:, :128] + weighted[:, 128:]
            cols_t += jnp.sum(w, axis=0, keepdims=True)
            cols_s += jnp.sum(weighted, axis=0, keepdims=True)
        tot[pl.ds(n, 1)] = cols_t
        wsum[pl.ds(n, 1)] = cols_s
        return carry

    lax.fori_loop(0, 8, block, 0)
    first = lax.broadcasted_iota(I32, (2 * ROWS, 128), 1) < 64
    fwd[...] = jnp.where(
        first, jnp.sum(acc_t[...], axis=1, keepdims=True), jnp.sum(acc_s[...], axis=1, keepdims=True)
    )
    for m in range(2):
        part = pl.ds(ROWS * m, ROWS)
        total = jnp.zeros((ROWS, WIDTH), F32)
        for n in range(8):
            total += jnp.dot(weight_bf[n, part], targets[n], preferred_element_type=F32)
        partner[part] = total


def score(idx, own, sib, halves):
    return pl.pallas_call(
        score_kernel,
        out_shape=(
            jax.ShapeDtypeStruct((8, 2 * ROWS, ROWS), F32),
            jax.ShapeDtypeStruct((2 * ROWS, 128), F32),
            jax.ShapeDtypeStruct((8, ROWS), F32),
            jax.ShapeDtypeStruct((8, ROWS), F32),
            jax.ShapeDtypeStruct((2 * ROWS, WIDTH), F32),
        ),
        in_specs=[sm(), vm(), vm()] + [hbm()] * 16,
        out_specs=(vm(),) * 5,
        scratch_shapes=[
            pltpu.VMEM((8, ROWS, WIDTH), BF16),
            pltpu.VMEM((2 * ROWS, WIDTH), BF16),
            pltpu.VMEM((8, 2 * ROWS, ROWS), BF16),
            pltpu.VMEM((2 * ROWS, 128), F32),
            pltpu.VMEM((2 * ROWS, 128), F32),
            pltpu.SemaphoreType.DMA((8,)),
        ],
        compiler_params=params(),
        cost_estimate=pl.CostEstimate(flops=2**33, bytes_accessed=12 * 2**20, transcendentals=2**20),
    )(idx, own, sib, *halves)


def fore_kernel(order, weight, mine, other, tot, wsum, payload):
    both = mine[...] + jnp.concatenate([other[ROWS:], other[:ROWS]], axis=0)
    stat = both[:, 64:65] / both[:, 0:1]
    for n in range(8):
        place = order[n]
        fore = jnp.sum(weight[n] * stat, axis=0, keepdims=True)
        payload[place, pl.ds(16, 1)] = fore
        t, s = tot[pl.ds(n, 1)], wsum[pl.ds(n, 1)]
        for d in range(8):
            payload[d, pl.ds(place, 1)] = t
            payload[d, pl.ds(8 + place, 1)] = s


def fore(order, weight, mine, other, tot, wsum):
    return pl.pallas_call(
        fore_kernel,
        out_shape=jax.ShapeDtypeStruct((8, 24, ROWS), F32),
        in_specs=[sm()] + [vm()] * 5,
        out_specs=vm(),
        compiler_params=params(),
        cost_estimate=pl.CostEstimate(flops=2**22, bytes_accessed=5 * 2**20, transcendentals=0),
    )(order, weight, mine, other, tot, wsum)


def back_kernel(order, weight, heard, back, target):
    sums = heard[0]
    for d in range(1, 8):
        sums = sums + heard[d]
    stat = sums[8:16] / sums[0:8]
    place = order[0]
    picked = lax.broadcasted_iota(I32, (8, ROWS), 0) == place
    own_total = jnp.sum(jnp.where(picked, sums[0:8], 0.0), axis=0, keepdims=True)
    own_stat = jnp.sum(jnp.where(picked, stat, 0.0), axis=0, keepdims=True)
    margin = own_stat - 0.5 * (own_stat + sums[16:17] / own_total)
    target[...] = jnp.transpose(jnp.broadcast_to(margin, (128, ROWS)))
    acc = jnp.zeros((2 * ROWS, 128), F32)
    for n in range(8):
        there = lax.broadcasted_iota(I32, (8, ROWS), 0) == order[n]
        row = jnp.sum(jnp.where(there, stat, 0.0), axis=0, keepdims=True)
        prod = weight[n] * row
        acc = acc + (prod[:, :128] + prod[:, 128:])
    back[...] = jnp.broadcast_to(jnp.sum(acc, axis=1, keepdims=True), (2 * ROWS, 128))


def back(order, weight, heard):
    return pl.pallas_call(
        back_kernel,
        out_shape=(jax.ShapeDtypeStruct((2 * ROWS, 128), F32), jax.ShapeDtypeStruct((ROWS, 128), F32)),
        in_specs=[sm(), vm(), vm()],
        out_specs=(vm(), vm()),
        compiler_params=params(),
        cost_estimate=pl.CostEstimate(flops=2**22, bytes_accessed=5 * 2**20, transcendentals=0),
    )(order, weight, heard)


def home_kernel(mine, other, partner, partner_in, back_ref, back_in, target, out):
    total = mine[...] + other[...]
    denom, stat = total[:, 0:1], total[:, 64:65] / total[:, 0:1]
    margin = stat - 0.5 * (stat + (back_ref[:, 0:1] + back_in[:, 0:1]) / denom)
    lane = lax.broadcasted_iota(I32, (ROWS, EXTRA), 1)
    value = jnp.where(lane < 2, margin, target[...])
    high = value.astype(BF16)
    low = (value - high.astype(F32)).astype(BF16)
    extra = jnp.where((lane & 1) == 0, high.astype(F32), low.astype(F32)).astype(BF16)
    rows = ((partner[...] + partner_in[...]) / denom).astype(BF16)
    for i in range(8):
        for z in range(2):
            place = pl.ds((2 * i + z) * 32, 32)
            out[place, pl.ds(0, WIDTH)] = rows[32 * i : 32 * i + 32]
            out[place, pl.ds(WIDTH, EXTRA)] = extra[32 * i : 32 * i + 32]


def home(mine, other, partner, partner_in, back_part, back_in, target):
    return pl.pallas_call(
        home_kernel,
        out_shape=jax.ShapeDtypeStruct((PACK, WIDTH + EXTRA), BF16),
        in_specs=[vm()] * 7,
        out_specs=vm(),
        compiler_params=params(),
        cost_estimate=pl.CostEstimate(flops=2**20, bytes_accessed=4 * 2**20, transcendentals=0),
    )(mine, other, partner, partner_in, back_part, back_in, target)


def finish_kernel(idx, src_labels, tgt_labels, got, partner, margins):
    src = route_matrix(src_labels[...], idx[0])
    tgt = route_matrix(tgt_labels[...], idx[0])
    contract = (((0,), (0,)), ((), ()))
    partner[...] = lax.dot_general(src, got[:, :WIDTH], contract, preferred_element_type=F32)
    extra = got[:, WIDTH:]
    by_src = lax.dot_general(extra, src, contract, preferred_element_type=F32)
    by_tgt = lax.dot_general(extra, tgt, contract, preferred_element_type=F32)
    margins[0:1] = by_src[0:1] + by_src[1:2]
    margins[1:2] = by_tgt[2:3] + by_tgt[3:4]


def finish(idx, src_labels, tgt_labels, got):
    return pl.pallas_call(
        finish_kernel,
        out_shape=(jax.ShapeDtypeStruct((ROWS, WIDTH), F32), jax.ShapeDtypeStruct((2, ROWS), F32)),
        in_specs=[sm(), vm(), vm(), vm()],
        out_specs=(vm(), vm()),
        compiler_params=params(),
        cost_estimate=pl.CostEstimate(flops=2 * PACK * ROWS * WIDTH, bytes_accessed=3 * 2**20, transcendentals=0),
    )(idx, src_labels, tgt_labels, got)


def route(packed):
    return lax.all_to_all(packed.reshape(16, 32, -1), ROUTE, 0, 0, tiled=True)


def merge(arrived):
    pairs = arrived.reshape(8, 2, 32, WIDTH)
    return (pairs[:, 0] + pairs[:, 1]).reshape(ROWS, WIDTH)


def gather_plane(rows):
    b0, b1 = rows[:128], rows[128:]
    p0, m1, z0 = lax.ppermute(b0, "x", RIGHT), lax.ppermute(b1, "x", LEFT), lax.ppermute(b0, "zl", SWAP)
    p1, m0, z1 = lax.ppermute(b1, "x", RIGHT), lax.ppermute(b0, "x", LEFT), lax.ppermute(b1, "zl", SWAP)
    x0, x1 = lax.ppermute(p0, "x", RIGHT), lax.ppermute(m1, "x", LEFT)
    zp0, zm0 = lax.ppermute(z0, "x", RIGHT), lax.ppermute(z0, "x", LEFT)
    zp1, zm1 = lax.ppermute(z1, "x", RIGHT), lax.ppermute(z1, "x", LEFT)
    zx0, zx1 = lax.ppermute(x0, "zl", SWAP), lax.ppermute(x1, "zl", SWAP)
    return [b0, b1, p0, p1, m0, m1, z0, z1, x0, x1, zp0, zp1, zm0, zm1, zx0, zx1]


def on_device(source, source_label, target, target_label):
    zl, x = lax.axis_index("zl"), lax.axis_index("x")
    idx = zl.reshape(1).astype(I32)
    src_labels, tgt_labels = source_label.reshape(1, ROWS), target_label.reshape(1, ROWS)
    places = [(0, 0), (0, 3), (0, 1), (1, 0), (0, 2), (1, 3), (1, 1), (1, 2)]
    order = jnp.stack([(zl + dz) % 2 * 4 + (x + dx) % 4 for dz, dx in places]).astype(I32)

    tgt_rows = merge(route(pack(idx, tgt_labels, target)))
    halves = gather_plane(tgt_rows)
    src_own = merge(route(pack(idx, src_labels, source)))
    src_sib = lax.ppermute(src_own, "c", SWAP)

    weight, fwd, tot, wsum, partner = score(idx, src_own, src_sib, halves)
    fwd_in = lax.ppermute(fwd, "c", SWAP)
    partner_in = lax.ppermute(partner[ROWS:], "c", SWAP)
    payload = fore(order, weight, fwd, fwd_in, tot, wsum)
    heard = lax.all_to_all(payload, PLANE, 0, 0, tiled=True)
    back_part, tgt_margin = back(order, weight, heard)
    back_in = lax.ppermute(back_part[ROWS:], "c", SWAP)
    packed = home(fwd[:ROWS], fwd_in[ROWS:], partner[:ROWS], partner_in, back_part[:ROWS], back_in, tgt_margin)
    got = route(packed).reshape(PACK, WIDTH + EXTRA)
    partner_out, margins = finish(idx, src_labels, tgt_labels, got)
    return (partner_out, margins[0], margins[1])


def solution(mesh):
    fine = Mesh(mesh.devices.reshape(2, 4, 2, 4, 2), AXES)
    return jax.shard_map(
        on_device,
        mesh=fine,
        in_specs=(P(AXES, None), P(AXES), P(AXES, None), P(AXES)),
        out_specs=(P(AXES, None), P(AXES), P(AXES)),
        check_vma=False,
    )
```

```python
from functools import partial

import jax
import jax.numpy as jnp
from jax import lax
from jax.experimental import pallas as pl
from jax.experimental.pallas import tpu as pltpu
from jax.sharding import Mesh, PartitionSpec as P

F32, BF16, I32 = jnp.float32, jnp.bfloat16, jnp.int32
SHARP = 12.0
WIDTH = 1024
ROWS = 256
SLOTS = 64
PACK = 512
SCALE = SHARP * 1.4426950408889634 / WIDTH
VMEM_LIMIT = 20 * 2**20
AXES = ("zh", "y", "zl", "x", "c")
ROUTE = ("zh", "y", "zl")
PLANE = ("zl", "x")
RIGHT = [(i, (i + 1) % 4) for i in range(4)]
LEFT = [(i, (i + 3) % 4) for i in range(4)]
SWAP = [(0, 1), (1, 0)]
PLACES = [(0, 0), (0, 3), (0, 1), (1, 0), (0, 2), (1, 3), (1, 1), (1, 2)]
EXTRA = 128


def params():
    return pltpu.CompilerParams(vmem_limit_bytes=VMEM_LIMIT)


def vm():
    return pl.BlockSpec(memory_space=pltpu.VMEM)


def hbm():
    return pl.BlockSpec(memory_space=pl.ANY)


def slot_row(labels, half):
    mine = lax.broadcasted_iota(I32, (8, ROWS), 0) == labels
    upper = lax.broadcasted_iota(I32, (ROWS, ROWS), 0) < lax.broadcasted_iota(I32, (ROWS, ROWS), 1)
    before = jnp.dot(mine.astype(BF16), upper.astype(BF16), preferred_element_type=F32)
    rank = jnp.sum(jnp.where(mine, before, 0.0), axis=0, keepdims=True).astype(I32)
    return labels * SLOTS + jnp.where(half == 0, rank, SLOTS - 1 - rank)


def route_matrix(labels, half):
    return (lax.broadcasted_iota(I32, (PACK, ROWS), 0) == slot_row(labels, half)).astype(BF16)


def position(place):
    dz, dx = PLACES[place]
    return (lax.axis_index("zl") + dz) % 2 * 4 + (lax.axis_index("x") + dx) % 4


def pack_kernel(labels, rows, *refs):
    out = refs[-1]
    values = rows[...].astype(F32)
    square = jnp.mean(values * values, axis=-1, keepdims=True)
    normed = (values * lax.rsqrt(square + 1e-06)).astype(BF16)
    slots = route_matrix(labels[...], lax.axis_index("zl"))
    out[...] = jnp.dot(slots, normed, preferred_element_type=F32).astype(BF16)


def pack(labels, rows, *after):
    return pl.pallas_call(
        pack_kernel,
        out_shape=jax.ShapeDtypeStruct((PACK, WIDTH), BF16),
        in_specs=[vm()] * 2 + [hbm()] * len(after),
        out_specs=vm(),
        compiler_params=params(),
        cost_estimate=pl.CostEstimate(flops=2 * PACK * ROWS * WIDTH, bytes_accessed=3 * 2**19, transcendentals=ROWS),
    )(labels, rows, *after).reshape(16, 32, WIDTH)


def merge_kernel(arrived, *refs):
    out = refs[-1]
    for i in range(8):
        out[pl.ds(32 * i, 32)] = arrived[2 * i] + arrived[2 * i + 1]


def merge(arrived, *after):
    return pl.pallas_call(
        merge_kernel,
        out_shape=jax.ShapeDtypeStruct((ROWS, WIDTH), BF16),
        in_specs=[vm()] + [hbm()] * len(after),
        out_specs=vm(),
        compiler_params=params(),
        cost_estimate=pl.CostEstimate(flops=2**18, bytes_accessed=3 * 2**19, transcendentals=0),
    )(arrived, *after)


def regroup_kernel(picks, *refs):
    outs = refs[len(refs) - len(picks) :]
    for out, halves in zip(outs, picks):
        for n, (which, half) in enumerate(halves):
            out[pl.ds(128 * n, 128)] = refs[which][pl.ds(128 * half, 128)]


def regroup(arrays, picks):
    return pl.pallas_call(
        partial(regroup_kernel, picks),
        out_shape=tuple(jax.ShapeDtypeStruct((128 * len(halves), WIDTH), BF16) for halves in picks),
        in_specs=[vm()] * len(arrays),
        out_specs=(vm(),) * len(picks),
        compiler_params=params(),
        cost_estimate=pl.CostEstimate(flops=0, bytes_accessed=2**20, transcendentals=0),
    )(*arrays)


def tie_kernel(value, after, out):
    del value, after, out


def tie(value, after):
    return pl.pallas_call(
        tie_kernel,
        out_shape=jax.ShapeDtypeStruct(value.shape, value.dtype),
        in_specs=[hbm(), hbm()],
        out_specs=hbm(),
        input_output_aliases={0: 0},
        compiler_params=params(),
    )(value, after)


def score_kernel(pieces, count, carry, last, own, sib, *refs):
    arrays, refs = refs[:count], refs[count:]
    blocks = len(pieces) // 2
    halves = [arrays[which].at[pl.ds(128 * half, 128)] for which, half in pieces]
    if carry:
        (total_in, sum_in, own_in, sib_in), refs = refs[:4], refs[4:]
    weight, tot, wsum, partner_own, partner_sib, *fwd, weight_bf = refs
    for m, rows in enumerate((own, sib)):
        part = pl.ds(ROWS * m, ROWS)
        acc_t = total_in[part] if carry else jnp.zeros((ROWS, 128), F32)
        acc_s = sum_in[part] if carry else jnp.zeros((ROWS, 128), F32)
        for n in range(blocks):
            block = jnp.concatenate([halves[2 * n][...], halves[2 * n + 1][...]], axis=0)
            inner = lax.dot_general(rows[...], block, (((1,), (1,)), ((), ())), preferred_element_type=F32)
            w = jnp.exp2(SCALE * inner)
            weighted = w * inner
            weight[n, part] = w
            weight_bf[part, pl.ds(ROWS * n, ROWS)] = w.astype(BF16)
            acc_t = acc_t + (w[:, :128] + w[:, 128:])
            acc_s = acc_s + (weighted[:, :128] + weighted[:, 128:])
            cols_t = jnp.sum(w, axis=0, keepdims=True)
            cols_s = jnp.sum(weighted, axis=0, keepdims=True)
            tot[pl.ds(n, 1)] = cols_t if m == 0 else tot[pl.ds(n, 1)] + cols_t
            wsum[pl.ds(n, 1)] = cols_s if m == 0 else wsum[pl.ds(n, 1)] + cols_s
        if last:
            acc_t = jnp.sum(acc_t, axis=1, keepdims=True)
            acc_s = jnp.sum(acc_s, axis=1, keepdims=True) * (1.0 / WIDTH)
            fwd[0][part] = jnp.where(lax.broadcasted_iota(I32, (ROWS, 128), 1) < 64, acc_t, acc_s)
        else:
            fwd[0][part] = acc_t
            fwd[1][part] = acc_s
    for c in range(4):
        cols = pl.ds(256 * c, 256)
        block = jnp.concatenate([half[:, cols] for half in halves], axis=0)
        for m, out in enumerate((partner_own, partner_sib)):
            value = jnp.dot(weight_bf[pl.ds(ROWS * m, ROWS)], block, preferred_element_type=F32)
            if carry:
                value = value + (own_in, sib_in)[m][:, cols]
            out[:, cols] = value


def score(own, sib, arrays, pieces, carry, last):
    blocks = len(pieces) // 2
    row_sums = 1 if last else 2
    return pl.pallas_call(
        partial(score_kernel, pieces, len(arrays), bool(carry), last),
        out_shape=(
            jax.ShapeDtypeStruct((blocks, 2 * ROWS, ROWS), F32),
            jax.ShapeDtypeStruct((blocks, ROWS), F32),
            jax.ShapeDtypeStruct((blocks, ROWS), F32),
            jax.ShapeDtypeStruct((ROWS, WIDTH), F32),
            jax.ShapeDtypeStruct((ROWS, WIDTH), F32),
        )
        + (jax.ShapeDtypeStruct((2 * ROWS, 128), F32),) * row_sums,
        in_specs=[vm()] * (2 + len(arrays) + len(carry)),
        out_specs=(vm(),) * (5 + row_sums),
        scratch_shapes=[pltpu.VMEM((2 * ROWS, ROWS * blocks), BF16)],
        compiler_params=params(),
        cost_estimate=pl.CostEstimate(
            flops=blocks * 2**29, bytes_accessed=blocks * 2**20 + 2**22, transcendentals=blocks * 2**17
        ),
    )(own, sib, *arrays, *carry)


def fore_kernel(mine, other, *refs):
    out, refs = refs[-1], refs[:-1]
    both = mine[...] + jnp.concatenate([other[ROWS:], other[:ROWS]], axis=0)
    stat = both[:, 64:65] / both[:, 0:1]
    place = 0
    for weight, tot, wsum in zip(refs[0::3], refs[1::3], refs[2::3]):
        for n in range(weight.shape[0]):
            at = position(place)
            out[0, pl.ds(at, 1)] = tot[pl.ds(n, 1)]
            out[0, pl.ds(8 + at, 1)] = wsum[pl.ds(n, 1)] * (1.0 / WIDTH)
            out[0, pl.ds(16 + at, 1)] = jnp.sum(weight[n] * stat, axis=0, keepdims=True)
            place += 1
    for d in range(1, 8):
        out[d] = out[0]


def fore(mine, other, parts):
    flat = [a for part in parts for a in part]
    return pl.pallas_call(
        fore_kernel,
        out_shape=jax.ShapeDtypeStruct((8, 24, ROWS), F32),
        in_specs=[vm()] * (2 + len(flat)),
        out_specs=vm(),
        compiler_params=params(),
        cost_estimate=pl.CostEstimate(flops=2**22, bytes_accessed=5 * 2**20, transcendentals=0),
    )(mine, other, *flat)


def back_kernel(heard, *refs):
    weights, (back_own, back_sib, target) = refs[:-3], refs[-3:]
    sums = heard[0]
    for d in range(1, 8):
        sums = sums + heard[d]
    stat = sums[8:16] / sums[0:8]
    row_of = lax.broadcasted_iota(I32, (8, ROWS), 0)

    def pick(values, at):
        return jnp.sum(jnp.where(row_of == at, values, 0.0), axis=0, keepdims=True)

    own_stat = pick(stat, position(0))
    mean = pick(sums[16:24], position(0)) / pick(sums[0:8], position(0))
    margin = own_stat - 0.5 * (own_stat + mean)
    target[...] = jnp.transpose(jnp.broadcast_to(margin, (128, ROWS)))
    acc = jnp.zeros((2 * ROWS, 128), F32)
    place = 0
    for weight in weights:
        for n in range(weight.shape[0]):
            prod = weight[n] * pick(stat, position(place))
            acc = acc + (prod[:, :128] + prod[:, 128:])
            place += 1
    total = jnp.broadcast_to(jnp.sum(acc, axis=1, keepdims=True), (2 * ROWS, 128))
    back_own[...] = total[:ROWS]
    back_sib[...] = total[ROWS:]


def back(heard, weights):
    return pl.pallas_call(
        back_kernel,
        out_shape=(jax.ShapeDtypeStruct((ROWS, 128), F32),) * 3,
        in_specs=[vm()] * (1 + len(weights)),
        out_specs=(vm(),) * 3,
        compiler_params=params(),
        cost_estimate=pl.CostEstimate(flops=2**22, bytes_accessed=5 * 2**20, transcendentals=0),
    )(heard, *weights)


def home_kernel(mine, other, partner, partner_in, back_own, back_in, target, out):
    total = mine[:ROWS] + other[ROWS:]
    denom = total[:, 0:1]
    stat = total[:, 64:65] / denom
    margin = stat - 0.5 * (stat + (back_own[:, 0:1] + back_in[:, 0:1]) / denom)
    lane = lax.broadcasted_iota(I32, (ROWS, EXTRA), 1)
    value = jnp.where(lane < 2, margin, target[...])
    high = value.astype(BF16).astype(F32)
    extra = jnp.where((lane & 1) == 0, high, value - high).astype(BF16)
    rows = ((partner[...] + partner_in[...]) / denom).astype(BF16)
    for i in range(8):
        for z in range(2):
            place = pl.ds((2 * i + z) * 32, 32)
            out[place, pl.ds(0, WIDTH)] = rows[32 * i : 32 * i + 32]
            out[place, pl.ds(WIDTH, EXTRA)] = extra[32 * i : 32 * i + 32]


def home(mine, other, partner, partner_in, back_own, back_in, target):
    return pl.pallas_call(
        home_kernel,
        out_shape=jax.ShapeDtypeStruct((PACK, WIDTH + EXTRA), BF16),
        in_specs=[vm()] * 7,
        out_specs=vm(),
        compiler_params=params(),
        cost_estimate=pl.CostEstimate(flops=2**20, bytes_accessed=3 * 2**20, transcendentals=0),
    )(mine, other, partner, partner_in, back_own, back_in, target)


def slots_kernel(src_labels, tgt_labels, src, tgt):
    for labels, out in ((src_labels, src), (tgt_labels, tgt)):
        slots = route_matrix(labels[...], lax.axis_index("zl")).astype(F32)
        out[...] = jnp.transpose(slots).astype(BF16)


def slots(src_labels, tgt_labels):
    return pl.pallas_call(
        slots_kernel,
        out_shape=(jax.ShapeDtypeStruct((ROWS, PACK), BF16),) * 2,
        in_specs=[vm()] * 2,
        out_specs=(vm(),) * 2,
        compiler_params=params(),
        cost_estimate=pl.CostEstimate(flops=2**24, bytes_accessed=2**19, transcendentals=0),
    )(src_labels, tgt_labels)


def unpack_kernel(src, tgt, got, extra, partner, src_out, tgt_out):
    partner[...] = jnp.dot(src[...], got[...], preferred_element_type=F32)

    @pl.when(pl.program_id(0) == 0)
    def _():
        for slots, first, out in ((src, 0, src_out), (tgt, 2, tgt_out)):
            found = jnp.transpose(jnp.dot(slots[...], extra[...], preferred_element_type=F32))
            out[...] = found[first : first + 1] + found[first + 1 : first + 2]


def unpack(src_slots, tgt_slots, got):
    whole = pl.BlockSpec((ROWS, PACK), lambda g: (0, 0))
    row = pl.BlockSpec((1, ROWS), lambda g: (0, 0))
    return pl.pallas_call(
        unpack_kernel,
        out_shape=(
            jax.ShapeDtypeStruct((ROWS, WIDTH), F32),
            jax.ShapeDtypeStruct((1, ROWS), F32),
            jax.ShapeDtypeStruct((1, ROWS), F32),
        ),
        grid=(4,),
        in_specs=[
            whole,
            whole,
            pl.BlockSpec((PACK, 256), lambda g: (0, g)),
            pl.BlockSpec((PACK, EXTRA), lambda g: (0, WIDTH // EXTRA)),
        ],
        out_specs=(pl.BlockSpec((ROWS, 256), lambda g: (0, g)), row, row),
        compiler_params=params(),
        cost_estimate=pl.CostEstimate(flops=2 * PACK * ROWS * WIDTH, bytes_accessed=2**21, transcendentals=0),
    )(src_slots, tgt_slots, got, got)


def route(packed):
    return lax.all_to_all(packed, ROUTE, 0, 0, tiled=True)


def on_device(source, source_label, target, target_label):
    src_labels, tgt_labels = source_label.reshape(1, ROWS), target_label.reshape(1, ROWS)
    src_slots, tgt_slots = slots(src_labels, tgt_labels)

    base = merge(route(pack(tgt_labels, target)))
    left, right = lax.ppermute(base, "x", RIGHT), lax.ppermute(base, "x", LEFT)
    across = lax.ppermute(base, "zl", SWAP)
    go_right, go_left = regroup((left, right), (((0, 0),), ((1, 1),)))
    far_first, far_second = lax.ppermute(go_right, "x", RIGHT), lax.ppermute(go_left, "x", LEFT)
    across_left, across_right = lax.ppermute(across, "x", RIGHT), lax.ppermute(across, "x", LEFT)
    (far,) = regroup((far_first, far_second), (((0, 0), (1, 0)),))
    last = lax.ppermute(far, "zl", SWAP)

    src_own = merge(route(pack(src_labels, source, base)), far_first, far_second)
    src_sib = lax.ppermute(src_own, "c", SWAP)
    calls = (
        (
            (base, left, right, across, far),
            ((0, 0), (0, 1), (1, 0), (1, 1), (2, 0), (2, 1), (3, 0), (3, 1), (4, 0), (4, 1)),
        ),
        (
            (across_left, across_right, last),
            ((0, 0), (0, 1), (1, 0), (1, 1), (2, 0), (2, 1)),
        ),
    )
    parts, carry = [], ()
    for n, (arrays, pieces) in enumerate(calls):
        weight, tot, wsum, own, sib, *fwd = score(src_own, src_sib, arrays, pieces, carry, n == 1)
        parts.append((weight, tot, wsum))
        carry = (*fwd, own, sib)
    (fwd,) = fwd
    fwd_in = lax.ppermute(fwd, "c", SWAP)
    partner_in = lax.ppermute(tie(sib, fwd_in), "c", SWAP)
    heard = lax.all_to_all(fore(fwd, fwd_in, parts), PLANE, 0, 0, tiled=True)
    back_own, back_sib, tgt_margin = back(heard, [part[0] for part in parts])
    back_in = lax.ppermute(back_sib, "c", SWAP)
    packed = home(fwd, fwd_in, own, partner_in, back_own, back_in, tgt_margin)
    got = route(packed.reshape(16, 32, -1)).reshape(PACK, WIDTH + EXTRA)
    partner_out, src_margin, tgt_margin = unpack(src_slots, tgt_slots, got)
    return (partner_out, src_margin.reshape(ROWS), tgt_margin.reshape(ROWS))


def solution(mesh):
    fine = Mesh(mesh.devices.reshape(2, 4, 2, 4, 2), AXES)
    return jax.shard_map(
        on_device,
        mesh=fine,
        in_specs=(P(AXES, None), P(AXES), P(AXES, None), P(AXES)),
        out_specs=(P(AXES, None), P(AXES), P(AXES)),
        check_vma=False,
    )
```

```python
from functools import partial

import jax
import jax.numpy as jnp
from jax import lax
from jax.experimental import pallas as pl
from jax.experimental.pallas import tpu as pltpu
from jax.sharding import Mesh, PartitionSpec as P

F32, BF16, I32 = jnp.float32, jnp.bfloat16, jnp.int32
SHARP = 12.0
WIDTH = 1024
ROWS = 256
SLOTS = 64
PACK = 512
SCALE = SHARP * 1.4426950408889634 / WIDTH
VMEM_LIMIT = 20 * 2**20
AXES = ("zh", "y", "zl", "x", "c")
ROUTE = ("zh", "y", "zl")
PLANE = ("zl", "x")
RIGHT = [(i, (i + 1) % 4) for i in range(4)]
LEFT = [(i, (i + 3) % 4) for i in range(4)]
SWAP = [(0, 1), (1, 0)]
PLACES = [(0, 0), (0, 3), (0, 1), (1, 0), (0, 2), (1, 3), (1, 1), (1, 2)]


def params():
    return pltpu.CompilerParams(vmem_limit_bytes=VMEM_LIMIT)


def vm():
    return pl.BlockSpec(memory_space=pltpu.VMEM)


def hbm():
    return pl.BlockSpec(memory_space=pl.ANY)


def slot_row(labels, half):
    mine = lax.broadcasted_iota(I32, (8, ROWS), 0) == labels
    upper = lax.broadcasted_iota(I32, (ROWS, ROWS), 0) < lax.broadcasted_iota(I32, (ROWS, ROWS), 1)
    before = jnp.dot(mine.astype(BF16), upper.astype(BF16), preferred_element_type=F32)
    rank = jnp.sum(jnp.where(mine, before, 0.0), axis=0, keepdims=True).astype(I32)
    return labels * SLOTS + jnp.where(half == 0, rank, SLOTS - 1 - rank)


def route_matrix(labels, half):
    return (lax.broadcasted_iota(I32, (PACK, ROWS), 0) == slot_row(labels, half)).astype(BF16)


def position(place):
    dz, dx = PLACES[place]
    return (lax.axis_index("zl") + dz) % 2 * 4 + (lax.axis_index("x") + dx) % 4


def pack_kernel(labels, rows, *refs):
    out = refs[-1]
    values = rows[...].astype(F32)
    square = jnp.mean(values * values, axis=-1, keepdims=True)
    normed = (values * lax.rsqrt(square + 1e-06)).astype(BF16)
    slots = route_matrix(labels[...], lax.axis_index("zl"))
    out[...] = jnp.dot(slots, normed, preferred_element_type=F32).astype(BF16)


def pack(labels, rows, *after):
    return pl.pallas_call(
        pack_kernel,
        out_shape=jax.ShapeDtypeStruct((PACK, WIDTH), BF16),
        in_specs=[vm()] * 2 + [hbm()] * len(after),
        out_specs=vm(),
        compiler_params=params(),
        cost_estimate=pl.CostEstimate(flops=2 * PACK * ROWS * WIDTH, bytes_accessed=3 * 2**19, transcendentals=ROWS),
    )(labels, rows, *after).reshape(16, 32, WIDTH)


def merge_kernel(arrived, *refs):
    out = refs[-1]
    for i in range(8):
        out[pl.ds(32 * i, 32)] = arrived[2 * i] + arrived[2 * i + 1]


def merge(arrived, *after):
    return pl.pallas_call(
        merge_kernel,
        out_shape=jax.ShapeDtypeStruct((ROWS, WIDTH), BF16),
        in_specs=[vm()] + [hbm()] * len(after),
        out_specs=vm(),
        compiler_params=params(),
        cost_estimate=pl.CostEstimate(flops=2**18, bytes_accessed=3 * 2**19, transcendentals=0),
    )(arrived, *after)


def regroup_kernel(picks, *refs):
    outs = refs[len(refs) - len(picks) :]
    for out, halves in zip(outs, picks):
        for n, (which, half) in enumerate(halves):
            out[pl.ds(128 * n, 128)] = refs[which][pl.ds(128 * half, 128)]


def regroup(arrays, picks):
    return pl.pallas_call(
        partial(regroup_kernel, picks),
        out_shape=tuple(jax.ShapeDtypeStruct((128 * len(halves), WIDTH), BF16) for halves in picks),
        in_specs=[vm()] * len(arrays),
        out_specs=(vm(),) * len(picks),
        compiler_params=params(),
        cost_estimate=pl.CostEstimate(flops=0, bytes_accessed=2**20, transcendentals=0),
    )(*arrays)


def score_kernel(pieces, count, carry, last, own, sib, *refs):
    arrays, refs = refs[:count], refs[count:]
    blocks = len(pieces) // 2
    halves = [arrays[which].at[pl.ds(128 * half, 128)] for which, half in pieces]
    if carry:
        (total_in, sum_in, own_in, sib_in), refs = refs[:4], refs[4:]
    weight, tot, wsum, partner_own, partner_sib, *fwd, weight_bf = refs
    for m, rows in enumerate((own, sib)):
        part = pl.ds(ROWS * m, ROWS)
        acc_t = total_in[part] if carry else jnp.zeros((ROWS, 128), F32)
        acc_s = sum_in[part] if carry else jnp.zeros((ROWS, 128), F32)
        for n in range(blocks):
            block = jnp.concatenate([halves[2 * n][...], halves[2 * n + 1][...]], axis=0)
            inner = lax.dot_general(rows[...], block, (((1,), (1,)), ((), ())), preferred_element_type=F32)
            w = jnp.exp2(SCALE * inner)
            weighted = w * inner
            weight[n, part] = w
            weight_bf[part, pl.ds(ROWS * n, ROWS)] = w.astype(BF16)
            acc_t = acc_t + (w[:, :128] + w[:, 128:])
            acc_s = acc_s + (weighted[:, :128] + weighted[:, 128:])
            cols_t = jnp.sum(w, axis=0, keepdims=True)
            cols_s = jnp.sum(weighted, axis=0, keepdims=True)
            tot[pl.ds(n, 1)] = cols_t if m == 0 else tot[pl.ds(n, 1)] + cols_t
            wsum[pl.ds(n, 1)] = cols_s if m == 0 else wsum[pl.ds(n, 1)] + cols_s
        if last:
            acc_t = jnp.sum(acc_t, axis=1, keepdims=True)
            acc_s = jnp.sum(acc_s, axis=1, keepdims=True) * (1.0 / WIDTH)
            fwd[0][part] = jnp.where(lax.broadcasted_iota(I32, (ROWS, 128), 1) < 64, acc_t, acc_s)
        else:
            fwd[0][part] = acc_t
            fwd[1][part] = acc_s
    for c in range(4):
        cols = pl.ds(256 * c, 256)
        block = jnp.concatenate([half[:, cols] for half in halves], axis=0)
        for m, out in enumerate((partner_own, partner_sib)):
            value = jnp.dot(weight_bf[pl.ds(ROWS * m, ROWS)], block, preferred_element_type=F32)
            if carry:
                value = value + (own_in, sib_in)[m][:, cols]
            out[:, cols] = value


def score(own, sib, arrays, pieces, carry, last):
    blocks = len(pieces) // 2
    row_sums = 1 if last else 2
    return pl.pallas_call(
        partial(score_kernel, pieces, len(arrays), bool(carry), last),
        out_shape=(
            jax.ShapeDtypeStruct((blocks, 2 * ROWS, ROWS), F32),
            jax.ShapeDtypeStruct((blocks, ROWS), F32),
            jax.ShapeDtypeStruct((blocks, ROWS), F32),
            jax.ShapeDtypeStruct((ROWS, WIDTH), F32),
            jax.ShapeDtypeStruct((ROWS, WIDTH), F32),
        )
        + (jax.ShapeDtypeStruct((2 * ROWS, 128), F32),) * row_sums,
        in_specs=[vm()] * (2 + len(arrays) + len(carry)),
        out_specs=(vm(),) * (5 + row_sums),
        scratch_shapes=[pltpu.VMEM((2 * ROWS, ROWS * blocks), BF16)],
        compiler_params=params(),
        cost_estimate=pl.CostEstimate(
            flops=blocks * 2**29, bytes_accessed=blocks * 2**20 + 2**22, transcendentals=blocks * 2**17
        ),
    )(own, sib, *arrays, *carry)


def fore_kernel(mine, other, after, *refs):
    del after
    out, refs = refs[-1], refs[:-1]
    both = mine[...] + jnp.concatenate([other[ROWS:], other[:ROWS]], axis=0)
    stat = both[:, 64:65] / both[:, 0:1]
    place = 0
    for weight, tot, wsum in zip(refs[0::3], refs[1::3], refs[2::3]):
        for n in range(weight.shape[0]):
            at = position(place)
            out[0, pl.ds(at, 1)] = tot[pl.ds(n, 1)]
            out[0, pl.ds(8 + at, 1)] = wsum[pl.ds(n, 1)] * (1.0 / WIDTH)
            out[0, pl.ds(16 + at, 1)] = jnp.sum(weight[n] * stat, axis=0, keepdims=True)
            place += 1
    for d in range(1, 8):
        out[d] = out[0]


def fore(mine, other, after, parts):
    flat = [a for part in parts for a in part]
    return pl.pallas_call(
        fore_kernel,
        out_shape=jax.ShapeDtypeStruct((8, 24, ROWS), F32),
        in_specs=[vm()] * 2 + [hbm()] + [vm()] * len(flat),
        out_specs=vm(),
        compiler_params=params(),
        cost_estimate=pl.CostEstimate(flops=2**22, bytes_accessed=5 * 2**20, transcendentals=0),
    )(mine, other, after, *flat)


def back_kernel(heard, *refs):
    weights, (back_own, back_sib, target) = refs[:-3], refs[-3:]
    sums = heard[0]
    for d in range(1, 8):
        sums = sums + heard[d]
    stat = sums[8:16] / sums[0:8]
    row_of = lax.broadcasted_iota(I32, (8, ROWS), 0)

    def pick(values, at):
        return jnp.sum(jnp.where(row_of == at, values, 0.0), axis=0, keepdims=True)

    own_stat = pick(stat, position(0))
    mean = pick(sums[16:24], position(0)) / pick(sums[0:8], position(0))
    margin = own_stat - 0.5 * (own_stat + mean)
    target[...] = margin
    acc = jnp.zeros((2 * ROWS, 128), F32)
    place = 0
    for weight in weights:
        for n in range(weight.shape[0]):
            prod = weight[n] * pick(stat, position(place))
            acc = acc + (prod[:, :128] + prod[:, 128:])
            place += 1
    total = jnp.broadcast_to(jnp.sum(acc, axis=1, keepdims=True), (2 * ROWS, 128))
    back_own[...] = total[:ROWS]
    back_sib[...] = total[ROWS:]


def back(heard, weights):
    return pl.pallas_call(
        back_kernel,
        out_shape=(
            jax.ShapeDtypeStruct((ROWS, 128), F32),
            jax.ShapeDtypeStruct((ROWS, 128), F32),
            jax.ShapeDtypeStruct((1, ROWS), F32),
        ),
        in_specs=[vm()] * (1 + len(weights)),
        out_specs=(vm(),) * 3,
        compiler_params=params(),
        cost_estimate=pl.CostEstimate(flops=2**22, bytes_accessed=5 * 2**20, transcendentals=0),
    )(heard, *weights)


def home_kernel(mine, other, partner, partner_in, *refs):
    outs, rows = refs[:4], refs[4]
    denom = mine[:ROWS, 0:1] + other[ROWS:, 0:1]
    rows[...] = ((partner[...] + partner_in[...]) / denom).astype(BF16)
    zh, y = lax.axis_index("zh"), lax.axis_index("y")
    for d in range(4):
        for u in range(2):
            block = ((zh + u) % 2) * 4 + (y + d) % 4
            outs[d][pl.ds(32 * u, 32)] = rows[pl.ds(pl.multiple_of(block * 32, 32), 32)]


def home(mine, other, partner, partner_in):
    return pl.pallas_call(
        home_kernel,
        out_shape=(jax.ShapeDtypeStruct((64, WIDTH), BF16),) * 4,
        in_specs=[vm()] * 4,
        out_specs=(vm(),) * 4,
        scratch_shapes=[pltpu.VMEM((ROWS, WIDTH), BF16)],
        compiler_params=params(),
        cost_estimate=pl.CostEstimate(flops=2**20, bytes_accessed=3 * 2**20, transcendentals=0),
    )(mine, other, partner, partner_in)


def turn_kernel(r0, r1, r2, r3, *outs):
    for u, out in enumerate(outs):
        for d, r in enumerate((r0, r1, r2, r3)):
            out[pl.ds(32 * d, 32)] = r[pl.ds(32 * u, 32)]


def turn(rows):
    return pl.pallas_call(
        turn_kernel,
        out_shape=(jax.ShapeDtypeStruct((128, WIDTH), BF16),) * 2,
        in_specs=[vm()] * 4,
        out_specs=(vm(),) * 2,
        compiler_params=params(),
        cost_estimate=pl.CostEstimate(flops=0, bytes_accessed=2**20, transcendentals=0),
    )(*rows)


def margin_kernel(mine, other, back_own, back_in, target, out):
    total = mine[:ROWS] + other[ROWS:]
    denom = total[:, 0:1]
    stat = total[:, 64:65] / denom
    margin = stat - 0.5 * (stat + (back_own[:, 0:1] + back_in[:, 0:1]) / denom)
    row = jnp.transpose(jnp.broadcast_to(margin, (ROWS, 128)))
    both = jnp.concatenate([row[0:1], target[...]], axis=0)
    for d in range(16):
        out[d] = both


def margins(mine, other, back_own, back_in, target):
    return pl.pallas_call(
        margin_kernel,
        out_shape=jax.ShapeDtypeStruct((16, 2, ROWS), F32),
        in_specs=[vm()] * 5,
        out_specs=vm(),
        compiler_params=params(),
        cost_estimate=pl.CostEstimate(flops=2**18, bytes_accessed=2**20, transcendentals=0),
    )(mine, other, back_own, back_in, target)


def slots_kernel(labels, out):
    zh, y, zl = lax.axis_index("zh"), lax.axis_index("y"), lax.axis_index("zl")
    slot = slot_row(labels[...], zl)
    bucket = slot >> 6
    peer = ((bucket >> 2) ^ zh) * 8 + (((slot >> 5) & 1) ^ zl) * 4 + ((y - (bucket & 3)) & 3)
    place = peer * 32 + (slot & 31)
    out[...] = jnp.transpose((lax.broadcasted_iota(I32, (PACK, ROWS), 0) == place).astype(F32)).astype(BF16)


def slots(labels):
    return pl.pallas_call(
        slots_kernel,
        out_shape=jax.ShapeDtypeStruct((ROWS, PACK), BF16),
        in_specs=[vm()],
        out_specs=vm(),
        compiler_params=params(),
        cost_estimate=pl.CostEstimate(flops=2**24, bytes_accessed=2**19, transcendentals=0),
    )(labels)


def unpack_kernel(place, g0, g1, g2, g3, partner, token):
    got = jnp.concatenate([g[...] for g in (g0, g1, g2, g3)], axis=0)
    partner[...] = jnp.dot(place[...], got, preferred_element_type=F32)
    token[...] = jnp.zeros_like(token)


def unpack(place, got):
    return pl.pallas_call(
        unpack_kernel,
        out_shape=(jax.ShapeDtypeStruct((ROWS, WIDTH), F32), jax.ShapeDtypeStruct((8, 128), F32)),
        grid=(4,),
        in_specs=[pl.BlockSpec((ROWS, PACK), lambda g: (0, 0))] + [pl.BlockSpec((128, 256), lambda g: (0, g))] * 4,
        out_specs=(pl.BlockSpec((ROWS, 256), lambda g: (0, g)), pl.BlockSpec((8, 128), lambda g: (0, 0))),
        compiler_params=params(),
        cost_estimate=pl.CostEstimate(flops=2 * PACK * ROWS * WIDTH, bytes_accessed=2**21, transcendentals=0),
    )(place, *got)


def finish_kernel(src_labels, tgt_labels, got, after, src_out, tgt_out):
    del after
    for kind, labels, out in ((0, src_labels, src_out), (1, tgt_labels, tgt_out)):
        slot = slot_row(labels[...], lax.axis_index("zl"))
        column = lax.axis_index(("zh", "y")) * 32 + (slot & 31)
        place = (lax.broadcasted_iota(I32, (ROWS, ROWS), 0) == column).astype(BF16)
        values = jnp.concatenate([got[s, kind : kind + 1] for s in range(16)], axis=0)
        found = jnp.zeros((16, ROWS), F32)
        for _ in range(3):
            piece = values.astype(BF16)
            values = values - piece.astype(F32)
            found = found + jnp.dot(piece, place, preferred_element_type=F32)
        here = lax.broadcasted_iota(I32, (16, ROWS), 0) == (slot >> 5)
        out[...] = jnp.sum(jnp.where(here, found, 0.0), axis=0, keepdims=True)


def finish(src_labels, tgt_labels, got, after):
    return pl.pallas_call(
        finish_kernel,
        out_shape=(jax.ShapeDtypeStruct((1, ROWS), F32),) * 2,
        in_specs=[vm()] * 3 + [hbm()],
        out_specs=(vm(), vm()),
        compiler_params=params(),
        cost_estimate=pl.CostEstimate(flops=2**24, bytes_accessed=2**16, transcendentals=0),
    )(src_labels, tgt_labels, got, after)


def route(packed):
    return lax.all_to_all(packed, ROUTE, 0, 0, tiled=True)


def shift(d):
    return [(i, (i + d) % 4) for i in range(4)]


def on_device(source, source_label, target, target_label):
    src_labels, tgt_labels = source_label.reshape(1, ROWS), target_label.reshape(1, ROWS)
    place = slots(src_labels)

    base = merge(route(pack(tgt_labels, target)))
    left, right = lax.ppermute(base, "x", RIGHT), lax.ppermute(base, "x", LEFT)
    across = lax.ppermute(base, "zl", SWAP)
    go_right, go_left = regroup((left, right), (((0, 0),), ((1, 1),)))
    far_first, far_second = lax.ppermute(go_right, "x", RIGHT), lax.ppermute(go_left, "x", LEFT)
    across_left, across_right = lax.ppermute(across, "x", RIGHT), lax.ppermute(across, "x", LEFT)
    (far,) = regroup((far_first, far_second), (((0, 0), (1, 0)),))
    last = lax.ppermute(far, "zl", SWAP)

    src_own = merge(route(pack(src_labels, source, base)), far_first, far_second)
    src_sib = lax.ppermute(src_own, "c", SWAP)
    calls = (
        (
            (base, left, right, across, far),
            ((0, 0), (0, 1), (1, 0), (1, 1), (2, 0), (2, 1), (3, 0), (3, 1), (4, 0), (4, 1)),
        ),
        (
            (across_left, across_right, last),
            ((0, 0), (0, 1), (1, 0), (1, 1), (2, 0), (2, 1)),
        ),
    )
    parts, carry = [], ()
    for n, (arrays, pieces) in enumerate(calls):
        weight, tot, wsum, own, sib, *fwd = score(src_own, src_sib, arrays, pieces, carry, n == 1)
        parts.append((weight, tot, wsum))
        carry = (*fwd, own, sib)
    (fwd,) = fwd
    fwd_in = lax.ppermute(fwd, "c", SWAP)
    partner_in = lax.ppermute(sib, "c", SWAP)

    by_y = home(fwd, fwd_in, own, partner_in)
    by_y = (by_y[0],) + tuple(lax.ppermute(by_y[d], "y", shift(d)) for d in (1, 2, 3))
    same, flip = turn(by_y)
    got = [same] + [
        lax.ppermute(rows, ("zh", "zl"), [(i, i ^ z) for i in range(4)]) for z, rows in ((1, same), (2, flip), (3, flip))
    ]
    partner_out, token = unpack(place, got)

    heard = lax.all_to_all(fore(fwd, fwd_in, by_y[0], parts), PLANE, 0, 0, tiled=True)
    back_own, back_sib, tgt_margin = back(heard, [part[0] for part in parts])
    back_in = lax.ppermute(back_sib, "c", SWAP)
    both = route(margins(fwd, fwd_in, back_own, back_in, tgt_margin))
    src_margin, tgt_margin = finish(src_labels, tgt_labels, both, token)
    return (partner_out, src_margin.reshape(ROWS), tgt_margin.reshape(ROWS))


def solution(mesh):
    fine = Mesh(mesh.devices.reshape(2, 4, 2, 4, 2), AXES)
    return jax.shard_map(
        on_device,
        mesh=fine,
        in_specs=(P(AXES, None), P(AXES), P(AXES, None), P(AXES)),
        out_specs=(P(AXES, None), P(AXES), P(AXES)),
        check_vma=False,
    )
```

```python
from functools import partial

import jax
import jax.numpy as jnp
from jax import lax
from jax.experimental import pallas as pl
from jax.experimental.pallas import tpu as pltpu
from jax.sharding import Mesh, PartitionSpec as P

F32, BF16, I32 = jnp.float32, jnp.bfloat16, jnp.int32
SHARP = 12.0
WIDTH = 1024
ROWS = 256
SLOTS = 64
PACK = 512
SCALE = SHARP * 1.4426950408889634 / WIDTH
VMEM_LIMIT = 20 * 2**20
AXES = ("zh", "y", "zl", "x", "c")
ROUTE = ("zh", "y", "zl")
PLANE = ("zl", "x")
RIGHT = [(i, (i + 1) % 4) for i in range(4)]
LEFT = [(i, (i + 3) % 4) for i in range(4)]
SWAP = [(0, 1), (1, 0)]
PLACES = [(0, 0), (0, 3), (0, 1), (1, 0), (0, 2), (1, 2), (1, 3), (1, 1)]


def params():
    return pltpu.CompilerParams(vmem_limit_bytes=VMEM_LIMIT)


def vm():
    return pl.BlockSpec(memory_space=pltpu.VMEM)


def hbm():
    return pl.BlockSpec(memory_space=pl.ANY)


def slot_row(labels, half):
    mine = lax.broadcasted_iota(I32, (8, ROWS), 0) == labels
    upper = lax.broadcasted_iota(I32, (ROWS, ROWS), 0) < lax.broadcasted_iota(I32, (ROWS, ROWS), 1)
    before = jnp.dot(mine.astype(BF16), upper.astype(BF16), preferred_element_type=F32)
    rank = jnp.sum(jnp.where(mine, before, 0.0), axis=0, keepdims=True).astype(I32)
    return labels * SLOTS + jnp.where(half == 0, rank, SLOTS - 1 - rank)


def route_matrix(labels, half):
    return (lax.broadcasted_iota(I32, (PACK, ROWS), 0) == slot_row(labels, half)).astype(BF16)


def position(place):
    dz, dx = PLACES[place]
    return (lax.axis_index("zl") + dz) % 2 * 4 + (lax.axis_index("x") + dx) % 4


def pack_kernel(labels, rows, *refs):
    out = refs[-1]
    values = rows[...].astype(F32)
    square = jnp.mean(values * values, axis=-1, keepdims=True)
    normed = (values * lax.rsqrt(square + 1e-06)).astype(BF16)
    slots = route_matrix(labels[...], lax.axis_index("zl"))
    out[...] = jnp.dot(slots, normed, preferred_element_type=F32).astype(BF16)


def pack(labels, rows, *after):
    return pl.pallas_call(
        pack_kernel,
        out_shape=jax.ShapeDtypeStruct((PACK, WIDTH), BF16),
        in_specs=[vm()] * 2 + [hbm()] * len(after),
        out_specs=vm(),
        compiler_params=params(),
        cost_estimate=pl.CostEstimate(flops=2 * PACK * ROWS * WIDTH, bytes_accessed=3 * 2**19, transcendentals=ROWS),
    )(labels, rows, *after).reshape(16, 32, WIDTH)


def merge_kernel(arrived, *refs):
    out = refs[-1]
    for i in range(8):
        out[pl.ds(32 * i, 32)] = arrived[2 * i] + arrived[2 * i + 1]


def merge(arrived, *after):
    return pl.pallas_call(
        merge_kernel,
        out_shape=jax.ShapeDtypeStruct((ROWS, WIDTH), BF16),
        in_specs=[vm()] + [hbm()] * len(after),
        out_specs=vm(),
        compiler_params=params(),
        cost_estimate=pl.CostEstimate(flops=2**18, bytes_accessed=3 * 2**19, transcendentals=0),
    )(arrived, *after)


def regroup_kernel(picks, *refs):
    outs = refs[len(refs) - len(picks) :]
    for out, halves in zip(outs, picks):
        for n, (which, half) in enumerate(halves):
            out[pl.ds(128 * n, 128)] = refs[which][pl.ds(128 * half, 128)]


def regroup(arrays, picks):
    return pl.pallas_call(
        partial(regroup_kernel, picks),
        out_shape=tuple(jax.ShapeDtypeStruct((128 * len(halves), WIDTH), BF16) for halves in picks),
        in_specs=[vm()] * len(arrays),
        out_specs=(vm(),) * len(picks),
        compiler_params=params(),
        cost_estimate=pl.CostEstimate(flops=0, bytes_accessed=2**20, transcendentals=0),
    )(*arrays)


def score_kernel(pieces, count, carry, last, own, sib, *refs):
    arrays, refs = refs[:count], refs[count:]
    blocks = len(pieces) // 2
    halves = [arrays[which].at[pl.ds(128 * half, 128)] for which, half in pieces]
    if carry:
        (total_in, sum_in, own_in, sib_in), refs = refs[:4], refs[4:]
    weight, tot, wsum, partner_own, partner_sib, *fwd, weight_bf = refs
    for m, rows in enumerate((own, sib)):
        part = pl.ds(ROWS * m, ROWS)
        acc_t = total_in[part] if carry else jnp.zeros((ROWS, 128), F32)
        acc_s = sum_in[part] if carry else jnp.zeros((ROWS, 128), F32)
        for n in range(blocks):
            block = jnp.concatenate([halves[2 * n][...], halves[2 * n + 1][...]], axis=0)
            inner = lax.dot_general(rows[...], block, (((1,), (1,)), ((), ())), preferred_element_type=F32)
            w = jnp.exp2(SCALE * inner)
            weighted = w * inner
            weight[n, part] = w
            weight_bf[part, pl.ds(ROWS * n, ROWS)] = w.astype(BF16)
            acc_t = acc_t + (w[:, :128] + w[:, 128:])
            acc_s = acc_s + (weighted[:, :128] + weighted[:, 128:])
            cols_t = jnp.sum(w, axis=0, keepdims=True)
            cols_s = jnp.sum(weighted, axis=0, keepdims=True)
            tot[pl.ds(n, 1)] = cols_t if m == 0 else tot[pl.ds(n, 1)] + cols_t
            wsum[pl.ds(n, 1)] = cols_s if m == 0 else wsum[pl.ds(n, 1)] + cols_s
        if last:
            acc_t = jnp.sum(acc_t, axis=1, keepdims=True)
            acc_s = jnp.sum(acc_s, axis=1, keepdims=True) * (1.0 / WIDTH)
            fwd[0][part] = jnp.where(lax.broadcasted_iota(I32, (ROWS, 128), 1) < 64, acc_t, acc_s)
        else:
            fwd[0][part] = acc_t
            fwd[1][part] = acc_s
    for c in range(4):
        cols = pl.ds(256 * c, 256)
        block = jnp.concatenate([half[:, cols] for half in halves], axis=0)
        for m, out in enumerate((partner_own, partner_sib)):
            value = jnp.dot(weight_bf[pl.ds(ROWS * m, ROWS)], block, preferred_element_type=F32)
            if carry:
                value = value + (own_in, sib_in)[m][:, cols]
            out[:, cols] = value.astype(out.dtype)


def score(own, sib, arrays, pieces, carry, last):
    blocks = len(pieces) // 2
    row_sums = 1 if last else 2
    return pl.pallas_call(
        partial(score_kernel, pieces, len(arrays), bool(carry), last),
        out_shape=(
            jax.ShapeDtypeStruct((blocks, 2 * ROWS, ROWS), F32),
            jax.ShapeDtypeStruct((blocks, ROWS), F32),
            jax.ShapeDtypeStruct((blocks, ROWS), F32),
            jax.ShapeDtypeStruct((ROWS, WIDTH), F32),
            jax.ShapeDtypeStruct((ROWS, WIDTH), BF16 if last else F32),
        )
        + (jax.ShapeDtypeStruct((2 * ROWS, 128), F32),) * row_sums,
        in_specs=[vm()] * (2 + len(arrays) + len(carry)),
        out_specs=(vm(),) * (5 + row_sums),
        scratch_shapes=[pltpu.VMEM((2 * ROWS, ROWS * blocks), BF16)],
        compiler_params=params(),
        cost_estimate=pl.CostEstimate(
            flops=blocks * 2**29, bytes_accessed=blocks * 2**20 + 2**22, transcendentals=blocks * 2**17
        ),
    )(own, sib, *arrays, *carry)


def fore_kernel(mine, other, after, *refs):
    del after
    out, refs = refs[-1], refs[:-1]
    both = mine[...] + jnp.concatenate([other[ROWS:], other[:ROWS]], axis=0)
    stat = both[:, 64:65] / both[:, 0:1]
    place = 0
    for weight, tot, wsum in zip(refs[0::3], refs[1::3], refs[2::3]):
        for n in range(weight.shape[0]):
            at = position(place)
            out[0, pl.ds(at, 1)] = tot[pl.ds(n, 1)]
            out[0, pl.ds(8 + at, 1)] = wsum[pl.ds(n, 1)] * (1.0 / WIDTH)
            out[0, pl.ds(16 + at, 1)] = jnp.sum(weight[n] * stat, axis=0, keepdims=True)
            place += 1
    for d in range(1, 8):
        out[d] = out[0]


def fore(mine, other, after, parts):
    flat = [a for part in parts for a in part]
    return pl.pallas_call(
        fore_kernel,
        out_shape=jax.ShapeDtypeStruct((8, 24, ROWS), F32),
        in_specs=[vm()] * 2 + [hbm()] + [vm()] * len(flat),
        out_specs=vm(),
        compiler_params=params(),
        cost_estimate=pl.CostEstimate(flops=2**22, bytes_accessed=5 * 2**20, transcendentals=0),
    )(mine, other, after, *flat)


def back_kernel(heard, *refs):
    weights, (back_own, back_sib, target) = refs[:-3], refs[-3:]
    sums = heard[0]
    for d in range(1, 8):
        sums = sums + heard[d]
    stat = sums[8:16] / sums[0:8]
    row_of = lax.broadcasted_iota(I32, (8, ROWS), 0)

    def pick(values, at):
        return jnp.sum(jnp.where(row_of == at, values, 0.0), axis=0, keepdims=True)

    own_stat = pick(stat, position(0))
    mean = pick(sums[16:24], position(0)) / pick(sums[0:8], position(0))
    margin = own_stat - 0.5 * (own_stat + mean)
    target[...] = margin
    acc = jnp.zeros((2 * ROWS, 128), F32)
    place = 0
    for weight in weights:
        for n in range(weight.shape[0]):
            prod = weight[n] * pick(stat, position(place))
            acc = acc + (prod[:, :128] + prod[:, 128:])
            place += 1
    total = jnp.broadcast_to(jnp.sum(acc, axis=1, keepdims=True), (2 * ROWS, 128))
    back_own[...] = total[:ROWS]
    back_sib[...] = total[ROWS:]


def back(heard, weights):
    return pl.pallas_call(
        back_kernel,
        out_shape=(
            jax.ShapeDtypeStruct((ROWS, 128), F32),
            jax.ShapeDtypeStruct((ROWS, 128), F32),
            jax.ShapeDtypeStruct((1, ROWS), F32),
        ),
        in_specs=[vm()] * (1 + len(weights)),
        out_specs=(vm(),) * 3,
        compiler_params=params(),
        cost_estimate=pl.CostEstimate(flops=2**22, bytes_accessed=5 * 2**20, transcendentals=0),
    )(heard, *weights)


def home_kernel(mine, other, partner, partner_in, *refs):
    outs, rows = refs[:4], refs[4]
    denom = mine[:ROWS, 0:1] + other[ROWS:, 0:1]
    rows[...] = ((partner[...] + partner_in[...].astype(F32)) / denom).astype(BF16)
    zh, y = lax.axis_index("zh"), lax.axis_index("y")
    for d in range(4):
        for u in range(2):
            block = ((zh + u) % 2) * 4 + (y + d) % 4
            outs[d][pl.ds(32 * u, 32)] = rows[pl.ds(pl.multiple_of(block * 32, 32), 32)]


def home(mine, other, partner, partner_in):
    return pl.pallas_call(
        home_kernel,
        out_shape=(jax.ShapeDtypeStruct((64, WIDTH), BF16),) * 4,
        in_specs=[vm()] * 4,
        out_specs=(vm(),) * 4,
        scratch_shapes=[pltpu.VMEM((ROWS, WIDTH), BF16)],
        compiler_params=params(),
        cost_estimate=pl.CostEstimate(flops=2**20, bytes_accessed=3 * 2**20, transcendentals=0),
    )(mine, other, partner, partner_in)


def turn_kernel(r0, r1, r2, r3, *outs):
    for u, out in enumerate(outs):
        for d, r in enumerate((r0, r1, r2, r3)):
            out[pl.ds(32 * d, 32)] = r[pl.ds(32 * u, 32)]


def turn(rows):
    return pl.pallas_call(
        turn_kernel,
        out_shape=(jax.ShapeDtypeStruct((128, WIDTH), BF16),) * 2,
        in_specs=[vm()] * 4,
        out_specs=(vm(),) * 2,
        compiler_params=params(),
        cost_estimate=pl.CostEstimate(flops=0, bytes_accessed=2**20, transcendentals=0),
    )(*rows)


def margin_kernel(mine, other, back_own, back_in, target, out):
    total = mine[:ROWS] + other[ROWS:]
    denom = total[:, 0:1]
    stat = total[:, 64:65] / denom
    margin = stat - 0.5 * (stat + (back_own[:, 0:1] + back_in[:, 0:1]) / denom)
    row = jnp.transpose(jnp.broadcast_to(margin, (ROWS, 128)))
    both = jnp.concatenate([row[0:1], target[...]], axis=0)
    for d in range(16):
        out[d] = both


def margins(mine, other, back_own, back_in, target):
    return pl.pallas_call(
        margin_kernel,
        out_shape=jax.ShapeDtypeStruct((16, 2, ROWS), F32),
        in_specs=[vm()] * 5,
        out_specs=vm(),
        compiler_params=params(),
        cost_estimate=pl.CostEstimate(flops=2**18, bytes_accessed=2**20, transcendentals=0),
    )(mine, other, back_own, back_in, target)


def slots_kernel(labels, out):
    zh, y, zl = lax.axis_index("zh"), lax.axis_index("y"), lax.axis_index("zl")
    slot = slot_row(labels[...], zl)
    bucket = slot >> 6
    peer = ((bucket >> 2) ^ zh) * 8 + (((slot >> 5) & 1) ^ zl) * 4 + ((y - (bucket & 3)) & 3)
    place = peer * 32 + (slot & 31)
    out[...] = jnp.transpose((lax.broadcasted_iota(I32, (PACK, ROWS), 0) == place).astype(F32)).astype(BF16)


def slots(labels):
    return pl.pallas_call(
        slots_kernel,
        out_shape=jax.ShapeDtypeStruct((ROWS, PACK), BF16),
        in_specs=[vm()],
        out_specs=vm(),
        compiler_params=params(),
        cost_estimate=pl.CostEstimate(flops=2**24, bytes_accessed=2**19, transcendentals=0),
    )(labels)


def unpack_kernel(place, g0, g1, g2, g3, partner, token):
    got = jnp.concatenate([g[...] for g in (g0, g1, g2, g3)], axis=0)
    partner[...] = jnp.dot(place[...], got, preferred_element_type=F32)
    token[...] = jnp.zeros_like(token)


def unpack(place, got):
    return pl.pallas_call(
        unpack_kernel,
        out_shape=(jax.ShapeDtypeStruct((ROWS, WIDTH), F32), jax.ShapeDtypeStruct((8, 128), F32)),
        in_specs=[vm()] * 5,
        out_specs=(vm(), vm()),
        compiler_params=params(),
        cost_estimate=pl.CostEstimate(flops=2 * PACK * ROWS * WIDTH, bytes_accessed=2**21, transcendentals=0),
    )(place, *got)


def finish_kernel(src_labels, tgt_labels, got, after, src_out, tgt_out):
    del after
    for kind, labels, out in ((0, src_labels, src_out), (1, tgt_labels, tgt_out)):
        slot = slot_row(labels[...], lax.axis_index("zl"))
        column = lax.axis_index(("zh", "y")) * 32 + (slot & 31)
        place = (lax.broadcasted_iota(I32, (ROWS, ROWS), 0) == column).astype(BF16)
        values = jnp.concatenate([got[s, kind : kind + 1] for s in range(16)], axis=0)
        found = jnp.zeros((16, ROWS), F32)
        for _ in range(3):
            piece = values.astype(BF16)
            values = values - piece.astype(F32)
            found = found + jnp.dot(piece, place, preferred_element_type=F32)
        here = lax.broadcasted_iota(I32, (16, ROWS), 0) == (slot >> 5)
        out[...] = jnp.sum(jnp.where(here, found, 0.0), axis=0, keepdims=True)


def finish(src_labels, tgt_labels, got, after):
    return pl.pallas_call(
        finish_kernel,
        out_shape=(jax.ShapeDtypeStruct((1, ROWS), F32),) * 2,
        in_specs=[vm()] * 3 + [hbm()],
        out_specs=(vm(), vm()),
        compiler_params=params(),
        cost_estimate=pl.CostEstimate(flops=2**24, bytes_accessed=2**16, transcendentals=0),
    )(src_labels, tgt_labels, got, after)


def route(packed):
    return lax.all_to_all(packed, ROUTE, 0, 0, tiled=True)


def shift(d):
    return [(i, (i + d) % 4) for i in range(4)]


def on_device(source, source_label, target, target_label):
    src_labels, tgt_labels = source_label.reshape(1, ROWS), target_label.reshape(1, ROWS)
    place = slots(src_labels)

    base = merge(route(pack(tgt_labels, target)))
    left, right = lax.ppermute(base, "x", RIGHT), lax.ppermute(base, "x", LEFT)
    across = lax.ppermute(base, "zl", SWAP)
    go_right, go_left = regroup((left, right), (((0, 0),), ((1, 1),)))
    far_first, far_second = lax.ppermute(go_right, "x", RIGHT), lax.ppermute(go_left, "x", LEFT)
    across_left, across_right = lax.ppermute(across, "x", RIGHT), lax.ppermute(across, "x", LEFT)
    (far,) = regroup((far_first, far_second), (((0, 0), (1, 0)),))
    last = lax.ppermute(far, "zl", SWAP)

    src_own = merge(route(pack(src_labels, source, base)), far_first, far_second)
    src_sib = lax.ppermute(src_own, "c", SWAP)
    calls = (
        (
            (base, left, right, across, far),
            ((0, 0), (0, 1), (1, 0), (1, 1), (2, 0), (2, 1), (3, 0), (3, 1), (4, 0), (4, 1)),
        ),
        (
            (last, across_left, across_right),
            ((0, 0), (0, 1), (1, 0), (1, 1), (2, 0), (2, 1)),
        ),
    )
    parts, carry = [], ()
    for n, (arrays, pieces) in enumerate(calls):
        weight, tot, wsum, own, sib, *fwd = score(src_own, src_sib, arrays, pieces, carry, n == 1)
        parts.append((weight, tot, wsum))
        carry = (*fwd, own, sib)
    (fwd,) = fwd
    fwd_in = lax.ppermute(fwd, "c", SWAP)
    partner_in = lax.ppermute(sib, "c", SWAP)

    by_y = home(fwd, fwd_in, own, partner_in)
    by_y = (by_y[0],) + tuple(lax.ppermute(by_y[d], "y", shift(d)) for d in (1, 2, 3))
    same, flip = turn(by_y)
    got = [same] + [
        lax.ppermute(rows, ("zh", "zl"), [(i, i ^ z) for i in range(4)]) for z, rows in ((1, same), (2, flip), (3, flip))
    ]
    partner_out, token = unpack(place, got)

    heard = lax.all_to_all(fore(fwd, fwd_in, by_y[0], parts), PLANE, 0, 0, tiled=True)
    back_own, back_sib, tgt_margin = back(heard, [part[0] for part in parts])
    back_in = lax.ppermute(back_sib, "c", SWAP)
    both = route(margins(fwd, fwd_in, back_own, back_in, tgt_margin))
    src_margin, tgt_margin = finish(src_labels, tgt_labels, both, token)
    return (partner_out, src_margin.reshape(ROWS), tgt_margin.reshape(ROWS))


def solution(mesh):
    fine = Mesh(mesh.devices.reshape(2, 4, 2, 4, 2), AXES)
    return jax.shard_map(
        on_device,
        mesh=fine,
        in_specs=(P(AXES, None), P(AXES), P(AXES, None), P(AXES)),
        out_specs=(P(AXES, None), P(AXES), P(AXES)),
        check_vma=False,
    )
```

```python
from functools import partial

import jax
import jax.numpy as jnp
from jax import lax
from jax.experimental import pallas as pl
from jax.experimental.pallas import tpu as pltpu
from jax.sharding import Mesh, PartitionSpec as P

F32, BF16, I32 = jnp.float32, jnp.bfloat16, jnp.int32
SHARP = 12.0
WIDTH = 1024
ROWS = 256
SLOTS = 64
PACK = 512
SCALE = SHARP * 1.4426950408889634 / WIDTH
VMEM_LIMIT = 20 * 2**20
AXES = ("zh", "y", "zl", "x", "c")
ROUTE = ("zh", "y", "zl")
PLANE = ("zl", "x")
RIGHT = [(i, (i + 1) % 4) for i in range(4)]
LEFT = [(i, (i + 3) % 4) for i in range(4)]
SWAP = [(0, 1), (1, 0)]
PLACES = [(0, 0), (0, 3), (0, 1), (1, 0), (0, 2), (1, 2), (1, 3), (1, 1)]


def params():
    return pltpu.CompilerParams(vmem_limit_bytes=VMEM_LIMIT)


def vm():
    return pl.BlockSpec(memory_space=pltpu.VMEM)


def hbm():
    return pl.BlockSpec(memory_space=pl.ANY)


def slot_row(labels, half):
    mine = lax.broadcasted_iota(I32, (8, ROWS), 0) == labels
    upper = lax.broadcasted_iota(I32, (ROWS, ROWS), 0) < lax.broadcasted_iota(I32, (ROWS, ROWS), 1)
    before = jnp.dot(mine.astype(BF16), upper.astype(BF16), preferred_element_type=F32)
    rank = jnp.sum(jnp.where(mine, before, 0.0), axis=0, keepdims=True).astype(I32)
    return labels * SLOTS + jnp.where(half == 0, rank, SLOTS - 1 - rank)


def route_matrix(labels, half):
    return (lax.broadcasted_iota(I32, (PACK, ROWS), 0) == slot_row(labels, half)).astype(BF16)


def position(place):
    dz, dx = PLACES[place]
    return (lax.axis_index("zl") + dz) % 2 * 4 + (lax.axis_index("x") + dx) % 4


def pack_kernel(labels, rows, *refs):
    out = refs[-1]
    values = rows[...].astype(F32)
    square = jnp.mean(values * values, axis=-1, keepdims=True)
    normed = (values * lax.rsqrt(square + 1e-06)).astype(BF16)
    slots = route_matrix(labels[...], lax.axis_index("zl"))
    out[...] = jnp.dot(slots, normed, preferred_element_type=F32).astype(BF16)


def pack(labels, rows, *after):
    return pl.pallas_call(
        pack_kernel,
        out_shape=jax.ShapeDtypeStruct((PACK, WIDTH), BF16),
        in_specs=[vm()] * 2 + [hbm()] * len(after),
        out_specs=vm(),
        compiler_params=params(),
        cost_estimate=pl.CostEstimate(flops=2 * PACK * ROWS * WIDTH, bytes_accessed=3 * 2**19, transcendentals=ROWS),
    )(labels, rows, *after).reshape(16, 32, WIDTH)


def merge_kernel(arrived, *refs):
    out = refs[-1]
    for i in range(8):
        out[pl.ds(32 * i, 32)] = arrived[2 * i] + arrived[2 * i + 1]


def merge(arrived, *after):
    return pl.pallas_call(
        merge_kernel,
        out_shape=jax.ShapeDtypeStruct((ROWS, WIDTH), BF16),
        in_specs=[vm()] + [hbm()] * len(after),
        out_specs=vm(),
        compiler_params=params(),
        cost_estimate=pl.CostEstimate(flops=2**18, bytes_accessed=3 * 2**19, transcendentals=0),
    )(arrived, *after)


def regroup_kernel(picks, *refs):
    outs = refs[len(refs) - len(picks) :]
    for out, halves in zip(outs, picks):
        for n, (which, half) in enumerate(halves):
            out[pl.ds(128 * n, 128)] = refs[which][pl.ds(128 * half, 128)]


def regroup(arrays, picks):
    return pl.pallas_call(
        partial(regroup_kernel, picks),
        out_shape=tuple(jax.ShapeDtypeStruct((128 * len(halves), WIDTH), BF16) for halves in picks),
        in_specs=[vm()] * len(arrays),
        out_specs=(vm(),) * len(picks),
        compiler_params=params(),
        cost_estimate=pl.CostEstimate(flops=0, bytes_accessed=2**20, transcendentals=0),
    )(*arrays)


def score_kernel(pieces, count, carry, last, own, sib, *refs):
    arrays, refs = refs[:count], refs[count:]
    blocks = len(pieces) // 2
    halves = [arrays[which].at[pl.ds(128 * half, 128)] for which, half in pieces]
    if carry:
        (total_in, sum_in, own_in, sib_in), refs = refs[:4], refs[4:]
    weight, tot, wsum, partner_own, partner_sib, *fwd, weight_bf = refs
    for m, rows in enumerate((own, sib)):
        part = pl.ds(ROWS * m, ROWS)
        acc_t = total_in[part] if carry else jnp.zeros((ROWS, 128), F32)
        acc_s = sum_in[part] if carry else jnp.zeros((ROWS, 128), F32)
        for n in range(blocks):
            block = jnp.concatenate([halves[2 * n][...], halves[2 * n + 1][...]], axis=0)
            inner = lax.dot_general(rows[...], block, (((1,), (1,)), ((), ())), preferred_element_type=F32)
            w = jnp.exp2(SCALE * inner)
            weighted = w * inner
            weight[n, part] = w
            weight_bf[part, pl.ds(ROWS * n, ROWS)] = w.astype(BF16)
            acc_t = acc_t + (w[:, :128] + w[:, 128:])
            acc_s = acc_s + (weighted[:, :128] + weighted[:, 128:])
            cols_t = jnp.sum(w, axis=0, keepdims=True)
            cols_s = jnp.sum(weighted, axis=0, keepdims=True)
            tot[pl.ds(n, 1)] = cols_t if m == 0 else tot[pl.ds(n, 1)] + cols_t
            wsum[pl.ds(n, 1)] = cols_s if m == 0 else wsum[pl.ds(n, 1)] + cols_s
        if last:
            acc_t = jnp.sum(acc_t, axis=1, keepdims=True)
            acc_s = jnp.sum(acc_s, axis=1, keepdims=True) * (1.0 / WIDTH)
            fwd[0][part] = jnp.where(lax.broadcasted_iota(I32, (ROWS, 128), 1) < 64, acc_t, acc_s)
        else:
            fwd[0][part] = acc_t
            fwd[1][part] = acc_s
    for c in range(4):
        cols = pl.ds(256 * c, 256)
        block = jnp.concatenate([half[:, cols] for half in halves], axis=0)
        for m, out in enumerate((partner_own, partner_sib)):
            value = jnp.dot(weight_bf[pl.ds(ROWS * m, ROWS)], block, preferred_element_type=F32)
            if carry:
                value = value + (own_in, sib_in)[m][:, cols]
            out[:, cols] = value.astype(out.dtype)


def score(own, sib, arrays, pieces, carry, last):
    blocks = len(pieces) // 2
    row_sums = 1 if last else 2
    return pl.pallas_call(
        partial(score_kernel, pieces, len(arrays), bool(carry), last),
        out_shape=(
            jax.ShapeDtypeStruct((blocks, 2 * ROWS, ROWS), F32),
            jax.ShapeDtypeStruct((blocks, ROWS), F32),
            jax.ShapeDtypeStruct((blocks, ROWS), F32),
            jax.ShapeDtypeStruct((ROWS, WIDTH), F32),
            jax.ShapeDtypeStruct((ROWS, WIDTH), BF16 if last else F32),
        )
        + (jax.ShapeDtypeStruct((2 * ROWS, 128), F32),) * row_sums,
        in_specs=[vm()] * (2 + len(arrays) + len(carry)),
        out_specs=(vm(),) * (5 + row_sums),
        scratch_shapes=[pltpu.VMEM((2 * ROWS, ROWS * blocks), BF16)],
        compiler_params=params(),
        cost_estimate=pl.CostEstimate(
            flops=blocks * 2**29, bytes_accessed=blocks * 2**20 + 2**22, transcendentals=blocks * 2**17
        ),
    )(own, sib, *arrays, *carry)


def fore_kernel(mine, other, after, *refs):
    del after
    out, refs = refs[-1], refs[:-1]
    both = mine[...] + jnp.concatenate([other[ROWS:], other[:ROWS]], axis=0)
    stat = both[:, 64:65] / both[:, 0:1]
    place = 0
    for weight, tot, wsum in zip(refs[0::3], refs[1::3], refs[2::3]):
        for n in range(weight.shape[0]):
            at = position(place)
            out[0, pl.ds(at, 1)] = tot[pl.ds(n, 1)]
            out[0, pl.ds(8 + at, 1)] = wsum[pl.ds(n, 1)] * (1.0 / WIDTH)
            out[0, pl.ds(16 + at, 1)] = jnp.sum(weight[n] * stat, axis=0, keepdims=True)
            place += 1
    for d in range(1, 8):
        out[d] = out[0]


def fore(mine, other, after, parts):
    flat = [a for part in parts for a in part]
    return pl.pallas_call(
        fore_kernel,
        out_shape=jax.ShapeDtypeStruct((8, 24, ROWS), F32),
        in_specs=[vm()] * 2 + [hbm()] + [vm()] * len(flat),
        out_specs=vm(),
        compiler_params=params(),
        cost_estimate=pl.CostEstimate(flops=2**22, bytes_accessed=5 * 2**20, transcendentals=0),
    )(mine, other, after, *flat)


def back_kernel(heard, *refs):
    weights, (back_own, back_sib, target) = refs[:-3], refs[-3:]
    sums = heard[0]
    for d in range(1, 8):
        sums = sums + heard[d]
    stat = sums[8:16] / sums[0:8]
    row_of = lax.broadcasted_iota(I32, (8, ROWS), 0)

    def pick(values, at):
        return jnp.sum(jnp.where(row_of == at, values, 0.0), axis=0, keepdims=True)

    own_stat = pick(stat, position(0))
    mean = pick(sums[16:24], position(0)) / pick(sums[0:8], position(0))
    margin = own_stat - 0.5 * (own_stat + mean)
    target[...] = margin
    acc = jnp.zeros((2 * ROWS, 128), F32)
    place = 0
    for weight in weights:
        for n in range(weight.shape[0]):
            prod = weight[n] * pick(stat, position(place))
            acc = acc + (prod[:, :128] + prod[:, 128:])
            place += 1
    total = jnp.broadcast_to(jnp.sum(acc, axis=1, keepdims=True), (2 * ROWS, 128))
    back_own[...] = total[:ROWS]
    back_sib[...] = total[ROWS:]


def back(heard, weights):
    return pl.pallas_call(
        back_kernel,
        out_shape=(
            jax.ShapeDtypeStruct((ROWS, 128), F32),
            jax.ShapeDtypeStruct((ROWS, 128), F32),
            jax.ShapeDtypeStruct((1, ROWS), F32),
        ),
        in_specs=[vm()] * (1 + len(weights)),
        out_specs=(vm(),) * 3,
        compiler_params=params(),
        cost_estimate=pl.CostEstimate(flops=2**22, bytes_accessed=5 * 2**20, transcendentals=0),
    )(heard, *weights)


def home_kernel(mine, other, partner, partner_in, *refs):
    outs, rows = refs[:4], refs[4]
    denom = mine[:ROWS, 0:1] + other[ROWS:, 0:1]
    rows[...] = ((partner[...] + partner_in[...].astype(F32)) / denom).astype(BF16)
    zh, y = lax.axis_index("zh"), lax.axis_index("y")
    for d in range(4):
        for u in range(2):
            block = ((zh + u) % 2) * 4 + (y + d) % 4
            outs[d][pl.ds(32 * u, 32)] = rows[pl.ds(pl.multiple_of(block * 32, 32), 32)]


def home(mine, other, partner, partner_in):
    return pl.pallas_call(
        home_kernel,
        out_shape=(jax.ShapeDtypeStruct((64, WIDTH), BF16),) * 4,
        in_specs=[vm()] * 4,
        out_specs=(vm(),) * 4,
        scratch_shapes=[pltpu.VMEM((ROWS, WIDTH), BF16)],
        compiler_params=params(),
        cost_estimate=pl.CostEstimate(flops=2**20, bytes_accessed=3 * 2**20, transcendentals=0),
    )(mine, other, partner, partner_in)


def turn_kernel(r0, r1, r2, r3, after, *outs):
    del after
    for u, out in enumerate(outs):
        for d, r in enumerate((r0, r1, r2, r3)):
            out[pl.ds(32 * d, 32)] = r[pl.ds(32 * u, 32)]


def turn(rows, after):
    return pl.pallas_call(
        turn_kernel,
        out_shape=(jax.ShapeDtypeStruct((128, WIDTH), BF16),) * 2,
        in_specs=[vm()] * 4 + [hbm()],
        out_specs=(vm(),) * 2,
        compiler_params=params(),
        cost_estimate=pl.CostEstimate(flops=0, bytes_accessed=2**20, transcendentals=0),
    )(*rows, after)


def margin_kernel(mine, other, back_own, back_in, target, out):
    total = mine[:ROWS] + other[ROWS:]
    denom = total[:, 0:1]
    stat = total[:, 64:65] / denom
    margin = stat - 0.5 * (stat + (back_own[:, 0:1] + back_in[:, 0:1]) / denom)
    row = jnp.transpose(jnp.broadcast_to(margin, (ROWS, 128)))
    both = jnp.concatenate([row[0:1], target[...]], axis=0)
    for d in range(16):
        out[d] = both


def margins(mine, other, back_own, back_in, target):
    return pl.pallas_call(
        margin_kernel,
        out_shape=jax.ShapeDtypeStruct((16, 2, ROWS), F32),
        in_specs=[vm()] * 5,
        out_specs=vm(),
        compiler_params=params(),
        cost_estimate=pl.CostEstimate(flops=2**18, bytes_accessed=2**20, transcendentals=0),
    )(mine, other, back_own, back_in, target)


def slots_kernel(labels, out):
    zh, y, zl = lax.axis_index("zh"), lax.axis_index("y"), lax.axis_index("zl")
    slot = slot_row(labels[...], zl)
    bucket = slot >> 6
    peer = ((bucket >> 2) ^ zh) * 8 + (((slot >> 5) & 1) ^ zl) * 4 + ((y - (bucket & 3)) & 3)
    place = peer * 32 + (slot & 31)
    out[...] = jnp.transpose((lax.broadcasted_iota(I32, (PACK, ROWS), 0) == place).astype(F32)).astype(BF16)


def slots(labels):
    return pl.pallas_call(
        slots_kernel,
        out_shape=jax.ShapeDtypeStruct((ROWS, PACK), BF16),
        in_specs=[vm()],
        out_specs=vm(),
        compiler_params=params(),
        cost_estimate=pl.CostEstimate(flops=2**24, bytes_accessed=2**19, transcendentals=0),
    )(labels)


def unpack_kernel(place, g0, g1, g2, g3, partner, token):
    got = jnp.concatenate([g[...] for g in (g0, g1, g2, g3)], axis=0)
    partner[...] = jnp.dot(place[...], got, preferred_element_type=F32)
    token[...] = jnp.zeros_like(token)


def unpack(place, got):
    return pl.pallas_call(
        unpack_kernel,
        out_shape=(jax.ShapeDtypeStruct((ROWS, WIDTH), F32), jax.ShapeDtypeStruct((8, 128), F32)),
        in_specs=[vm()] * 5,
        out_specs=(vm(), vm()),
        compiler_params=params(),
        cost_estimate=pl.CostEstimate(flops=2 * PACK * ROWS * WIDTH, bytes_accessed=2**21, transcendentals=0),
    )(place, *got)


def finish_kernel(src_labels, tgt_labels, got, after, src_out, tgt_out):
    del after
    for kind, labels, out in ((0, src_labels, src_out), (1, tgt_labels, tgt_out)):
        slot = slot_row(labels[...], lax.axis_index("zl"))
        column = lax.axis_index(("zh", "y")) * 32 + (slot & 31)
        place = (lax.broadcasted_iota(I32, (ROWS, ROWS), 0) == column).astype(BF16)
        values = jnp.concatenate([got[s, kind : kind + 1] for s in range(16)], axis=0)
        found = jnp.zeros((16, ROWS), F32)
        for _ in range(3):
            piece = values.astype(BF16)
            values = values - piece.astype(F32)
            found = found + jnp.dot(piece, place, preferred_element_type=F32)
        here = lax.broadcasted_iota(I32, (16, ROWS), 0) == (slot >> 5)
        out[...] = jnp.sum(jnp.where(here, found, 0.0), axis=0, keepdims=True)


def finish(src_labels, tgt_labels, got, after):
    return pl.pallas_call(
        finish_kernel,
        out_shape=(jax.ShapeDtypeStruct((1, ROWS), F32),) * 2,
        in_specs=[vm()] * 3 + [hbm()],
        out_specs=(vm(), vm()),
        compiler_params=params(),
        cost_estimate=pl.CostEstimate(flops=2**24, bytes_accessed=2**16, transcendentals=0),
    )(src_labels, tgt_labels, got, after)


def route(packed):
    return lax.all_to_all(packed, ROUTE, 0, 0, tiled=True)


def shift(d):
    return [(i, (i + d) % 4) for i in range(4)]


def on_device(source, source_label, target, target_label):
    src_labels, tgt_labels = source_label.reshape(1, ROWS), target_label.reshape(1, ROWS)
    place = slots(src_labels)

    base = merge(route(pack(tgt_labels, target)))
    left, right = lax.ppermute(base, "x", RIGHT), lax.ppermute(base, "x", LEFT)
    across = lax.ppermute(base, "zl", SWAP)
    go_right, go_left = regroup((left, right), (((0, 0),), ((1, 1),)))
    far_first, far_second = lax.ppermute(go_right, "x", RIGHT), lax.ppermute(go_left, "x", LEFT)
    across_left, across_right = lax.ppermute(across, "x", RIGHT), lax.ppermute(across, "x", LEFT)
    (far,) = regroup((far_first, far_second), (((0, 0), (1, 0)),))
    last = lax.ppermute(far, "zl", SWAP)

    src_own = merge(route(pack(src_labels, source, base)), far_first, far_second)
    src_sib = lax.ppermute(src_own, "c", SWAP)
    calls = (
        (
            (base, left, right, across, far),
            ((0, 0), (0, 1), (1, 0), (1, 1), (2, 0), (2, 1), (3, 0), (3, 1), (4, 0), (4, 1)),
        ),
        (
            (last, across_left, across_right),
            ((0, 0), (0, 1), (1, 0), (1, 1), (2, 0), (2, 1)),
        ),
    )
    parts, carry = [], ()
    for n, (arrays, pieces) in enumerate(calls):
        weight, tot, wsum, own, sib, *fwd = score(src_own, src_sib, arrays, pieces, carry, n == 1)
        parts.append((weight, tot, wsum))
        carry = (*fwd, own, sib)
    (fwd,) = fwd
    fwd_in = lax.ppermute(fwd, "c", SWAP)
    partner_in = lax.ppermute(sib, "c", SWAP)

    by_y = home(fwd, fwd_in, own, partner_in)
    by_y = (by_y[0],) + tuple(lax.ppermute(by_y[d], "y", shift(d)) for d in (1, 2, 3))
    heard = lax.all_to_all(fore(fwd, fwd_in, by_y[0], parts), PLANE, 0, 0, tiled=True)
    back_own, back_sib, tgt_margin = back(heard, [part[0] for part in parts])
    same, flip = turn(by_y, tgt_margin)
    got = [same] + [
        lax.ppermute(rows, ("zh", "zl"), [(i, i ^ z) for i in range(4)]) for z, rows in ((1, same), (2, flip), (3, flip))
    ]
    partner_out, token = unpack(place, got)

    back_in = lax.ppermute(back_sib, "c", SWAP)
    both = route(margins(fwd, fwd_in, back_own, back_in, tgt_margin))
    src_margin, tgt_margin = finish(src_labels, tgt_labels, both, token)
    return (partner_out, src_margin.reshape(ROWS), tgt_margin.reshape(ROWS))


def solution(mesh):
    fine = Mesh(mesh.devices.reshape(2, 4, 2, 4, 2), AXES)
    return jax.shard_map(
        on_device,
        mesh=fine,
        in_specs=(P(AXES, None), P(AXES), P(AXES, None), P(AXES)),
        out_specs=(P(AXES, None), P(AXES), P(AXES)),
        check_vma=False,
    )
```

```python
from functools import partial

import jax
import jax.numpy as jnp
from jax import lax
from jax.experimental import pallas as pl
from jax.experimental.pallas import tpu as pltpu
from jax.sharding import Mesh, PartitionSpec as P

F32, BF16, I32 = jnp.float32, jnp.bfloat16, jnp.int32
SHARP = 12.0
WIDTH = 1024
ROWS = 256
SLOTS = 64
PACK = 512
SCALE = SHARP * 1.4426950408889634 / WIDTH
VMEM_LIMIT = 20 * 2**20
AXES = ("zh", "y", "zl", "x", "c")
ROUTE = ("zh", "y", "zl")
PLANE = ("zl", "x")
RIGHT = [(i, (i + 1) % 4) for i in range(4)]
LEFT = [(i, (i + 3) % 4) for i in range(4)]
SWAP = [(0, 1), (1, 0)]
PLACES = [(0, 0), (0, 3), (0, 1), (1, 0), (0, 2), (1, 2), (1, 3), (1, 1)]


def params():
    return pltpu.CompilerParams(vmem_limit_bytes=VMEM_LIMIT)


def vm():
    return pl.BlockSpec(memory_space=pltpu.VMEM)


def hbm():
    return pl.BlockSpec(memory_space=pl.ANY)


def slot_row(labels, half):
    mine = lax.broadcasted_iota(I32, (8, ROWS), 0) == labels
    upper = lax.broadcasted_iota(I32, (ROWS, ROWS), 0) < lax.broadcasted_iota(I32, (ROWS, ROWS), 1)
    before = jnp.dot(mine.astype(BF16), upper.astype(BF16), preferred_element_type=F32)
    rank = jnp.sum(jnp.where(mine, before, 0.0), axis=0, keepdims=True).astype(I32)
    return labels * SLOTS + jnp.where(half == 0, rank, SLOTS - 1 - rank)


def route_matrix(labels, half):
    return (lax.broadcasted_iota(I32, (PACK, ROWS), 0) == slot_row(labels, half)).astype(BF16)


def position(place):
    dz, dx = PLACES[place]
    return (lax.axis_index("zl") + dz) % 2 * 4 + (lax.axis_index("x") + dx) % 4


def pack_kernel(labels, rows, *refs):
    out = refs[-1]
    values = rows[...].astype(F32)
    square = jnp.mean(values * values, axis=-1, keepdims=True)
    normed = (values * lax.rsqrt(square + 1e-06)).astype(BF16)
    slots = route_matrix(labels[...], lax.axis_index("zl"))
    out[...] = jnp.dot(slots, normed, preferred_element_type=F32).astype(BF16)


def pack(labels, rows, *after):
    return pl.pallas_call(
        pack_kernel,
        out_shape=jax.ShapeDtypeStruct((PACK, WIDTH), BF16),
        in_specs=[vm()] * 2 + [hbm()] * len(after),
        out_specs=vm(),
        compiler_params=params(),
        cost_estimate=pl.CostEstimate(flops=2 * PACK * ROWS * WIDTH, bytes_accessed=3 * 2**19, transcendentals=ROWS),
    )(labels, rows, *after).reshape(16, 32, WIDTH)


def merge_kernel(arrived, *refs):
    out = refs[-1]
    for i in range(8):
        out[pl.ds(32 * i, 32)] = arrived[2 * i] + arrived[2 * i + 1]


def merge(arrived, *after):
    return pl.pallas_call(
        merge_kernel,
        out_shape=jax.ShapeDtypeStruct((ROWS, WIDTH), BF16),
        in_specs=[vm()] + [hbm()] * len(after),
        out_specs=vm(),
        compiler_params=params(),
        cost_estimate=pl.CostEstimate(flops=2**18, bytes_accessed=3 * 2**19, transcendentals=0),
    )(arrived, *after)


def regroup_kernel(picks, *refs):
    outs = refs[len(refs) - len(picks) :]
    for out, halves in zip(outs, picks):
        for n, (which, half) in enumerate(halves):
            out[pl.ds(128 * n, 128)] = refs[which][pl.ds(128 * half, 128)]


def regroup(arrays, picks):
    return pl.pallas_call(
        partial(regroup_kernel, picks),
        out_shape=tuple(jax.ShapeDtypeStruct((128 * len(halves), WIDTH), BF16) for halves in picks),
        in_specs=[vm()] * len(arrays),
        out_specs=(vm(),) * len(picks),
        compiler_params=params(),
        cost_estimate=pl.CostEstimate(flops=0, bytes_accessed=2**20, transcendentals=0),
    )(*arrays)


def score_kernel(pieces, count, carry, last, own, sib, *refs):
    arrays, refs = refs[:count], refs[count:]
    blocks = len(pieces) // 2
    halves = [arrays[which].at[pl.ds(128 * half, 128)] for which, half in pieces]
    if carry:
        (total_in, sum_in, own_in, sib_in), refs = refs[:4], refs[4:]
    weight, tot, wsum, partner_own, partner_sib, *fwd, weight_bf = refs
    for m, rows in enumerate((own, sib)):
        part = pl.ds(ROWS * m, ROWS)
        acc_t = total_in[part] if carry else jnp.zeros((ROWS, 128), F32)
        acc_s = sum_in[part] if carry else jnp.zeros((ROWS, 128), F32)
        for n in range(blocks):
            block = jnp.concatenate([halves[2 * n][...], halves[2 * n + 1][...]], axis=0)
            inner = lax.dot_general(rows[...], block, (((1,), (1,)), ((), ())), preferred_element_type=F32)
            w = jnp.exp2(SCALE * inner)
            weighted = w * inner
            weight[n, part] = w
            weight_bf[part, pl.ds(ROWS * n, ROWS)] = w.astype(BF16)
            acc_t = acc_t + (w[:, :128] + w[:, 128:])
            acc_s = acc_s + (weighted[:, :128] + weighted[:, 128:])
            cols_t = jnp.sum(w, axis=0, keepdims=True)
            cols_s = jnp.sum(weighted, axis=0, keepdims=True)
            tot[pl.ds(n, 1)] = cols_t if m == 0 else tot[pl.ds(n, 1)] + cols_t
            wsum[pl.ds(n, 1)] = cols_s if m == 0 else wsum[pl.ds(n, 1)] + cols_s
        if last:
            acc_t = jnp.sum(acc_t, axis=1, keepdims=True)
            acc_s = jnp.sum(acc_s, axis=1, keepdims=True) * (1.0 / WIDTH)
            fwd[0][part] = jnp.where(lax.broadcasted_iota(I32, (ROWS, 128), 1) < 64, acc_t, acc_s)
        else:
            fwd[0][part] = acc_t
            fwd[1][part] = acc_s
    for c in range(4):
        cols = pl.ds(256 * c, 256)
        block = jnp.concatenate([half[:, cols] for half in halves], axis=0)
        for m, out in enumerate((partner_own, partner_sib)):
            value = jnp.dot(weight_bf[pl.ds(ROWS * m, ROWS)], block, preferred_element_type=F32)
            if carry:
                value = value + (own_in, sib_in)[m][:, cols]
            out[:, cols] = value.astype(out.dtype)


def score(own, sib, arrays, pieces, carry, last):
    blocks = len(pieces) // 2
    row_sums = 1 if last else 2
    return pl.pallas_call(
        partial(score_kernel, pieces, len(arrays), bool(carry), last),
        out_shape=(
            jax.ShapeDtypeStruct((blocks, 2 * ROWS, ROWS), F32),
            jax.ShapeDtypeStruct((blocks, ROWS), F32),
            jax.ShapeDtypeStruct((blocks, ROWS), F32),
            jax.ShapeDtypeStruct((ROWS, WIDTH), F32),
            jax.ShapeDtypeStruct((ROWS, WIDTH), BF16 if last else F32),
        )
        + (jax.ShapeDtypeStruct((2 * ROWS, 128), F32),) * row_sums,
        in_specs=[vm()] * (2 + len(arrays) + len(carry)),
        out_specs=(vm(),) * (5 + row_sums),
        scratch_shapes=[pltpu.VMEM((2 * ROWS, ROWS * blocks), BF16)],
        compiler_params=params(),
        cost_estimate=pl.CostEstimate(
            flops=blocks * 2**29, bytes_accessed=blocks * 2**20 + 2**22, transcendentals=blocks * 2**17
        ),
    )(own, sib, *arrays, *carry)


def fore_kernel(mine, other, after, *refs):
    del after
    out, refs = refs[-1], refs[:-1]
    both = mine[...] + jnp.concatenate([other[ROWS:], other[:ROWS]], axis=0)
    stat = both[:, 64:65] / both[:, 0:1]
    place = 0
    for weight, tot, wsum in zip(refs[0::3], refs[1::3], refs[2::3]):
        for n in range(weight.shape[0]):
            at = position(place)
            out[0, pl.ds(at, 1)] = tot[pl.ds(n, 1)]
            out[0, pl.ds(8 + at, 1)] = wsum[pl.ds(n, 1)] * (1.0 / WIDTH)
            out[0, pl.ds(16 + at, 1)] = jnp.sum(weight[n] * stat, axis=0, keepdims=True)
            place += 1
    for d in range(1, 8):
        out[d] = out[0]


def fore(mine, other, after, parts):
    flat = [a for part in parts for a in part]
    return pl.pallas_call(
        fore_kernel,
        out_shape=jax.ShapeDtypeStruct((8, 24, ROWS), F32),
        in_specs=[vm()] * 2 + [hbm()] + [vm()] * len(flat),
        out_specs=vm(),
        compiler_params=params(),
        cost_estimate=pl.CostEstimate(flops=2**22, bytes_accessed=5 * 2**20, transcendentals=0),
    )(mine, other, after, *flat)


def pick(values, at):
    here = lax.broadcasted_iota(I32, (8, ROWS), 0) == at
    return jnp.sum(jnp.where(here, values, 0.0), axis=0, keepdims=True)


def back_rows(acc, weight, stat, first):
    for n in range(weight.shape[0]):
        prod = weight[n] * pick(stat, position(first + n))
        acc = acc + (prod[:, :128] + prod[:, 128:])
    return acc


def back_kernel(heard, weight, acc, stat_out, target):
    sums = heard[0]
    for d in range(1, 8):
        sums = sums + heard[d]
    stat = sums[8:16] / sums[0:8]
    stat_out[...] = stat
    own_stat = pick(stat, position(0))
    mean = pick(sums[16:24], position(0)) / pick(sums[0:8], position(0))
    target[...] = own_stat - 0.5 * (own_stat + mean)
    acc[...] = back_rows(jnp.zeros((2 * ROWS, 128), F32), weight, stat, 0)


def back_last_kernel(acc, stat, weight, back_own, back_sib):
    total = back_rows(acc[...], weight, stat[...], 8 - weight.shape[0])
    total = jnp.broadcast_to(jnp.sum(total, axis=1, keepdims=True), (2 * ROWS, 128))
    back_own[...] = total[:ROWS]
    back_sib[...] = total[ROWS:]


def back(heard, early, late):
    acc, stat, target = pl.pallas_call(
        back_kernel,
        out_shape=(
            jax.ShapeDtypeStruct((2 * ROWS, 128), F32),
            jax.ShapeDtypeStruct((8, ROWS), F32),
            jax.ShapeDtypeStruct((1, ROWS), F32),
        ),
        in_specs=[vm()] * 2,
        out_specs=(vm(),) * 3,
        compiler_params=params(),
        cost_estimate=pl.CostEstimate(flops=2**21, bytes_accessed=3 * 2**20, transcendentals=0),
    )(heard, early)
    back_own, back_sib = pl.pallas_call(
        back_last_kernel,
        out_shape=(jax.ShapeDtypeStruct((ROWS, 128), F32),) * 2,
        in_specs=[vm()] * 3,
        out_specs=(vm(),) * 2,
        compiler_params=params(),
        cost_estimate=pl.CostEstimate(flops=2**21, bytes_accessed=2**21, transcendentals=0),
    )(acc, stat, late)
    return back_own, back_sib, target


def home_kernel(mine, other, partner, partner_in, *refs):
    outs, rows = refs[:4], refs[4]
    denom = mine[:ROWS, 0:1] + other[ROWS:, 0:1]
    rows[...] = ((partner[...] + partner_in[...].astype(F32)) / denom).astype(BF16)
    zh, y = lax.axis_index("zh"), lax.axis_index("y")
    for d in range(4):
        for u in range(2):
            block = ((zh + u) % 2) * 4 + (y + d) % 4
            outs[d][pl.ds(32 * u, 32)] = rows[pl.ds(pl.multiple_of(block * 32, 32), 32)]


def home(mine, other, partner, partner_in):
    return pl.pallas_call(
        home_kernel,
        out_shape=(jax.ShapeDtypeStruct((64, WIDTH), BF16),) * 4,
        in_specs=[vm()] * 4,
        out_specs=(vm(),) * 4,
        scratch_shapes=[pltpu.VMEM((ROWS, WIDTH), BF16)],
        compiler_params=params(),
        cost_estimate=pl.CostEstimate(flops=2**20, bytes_accessed=3 * 2**20, transcendentals=0),
    )(mine, other, partner, partner_in)


def turn_kernel(r0, r1, r2, r3, *outs):
    for u, out in enumerate(outs):
        for d, r in enumerate((r0, r1, r2, r3)):
            out[pl.ds(32 * d, 32)] = r[pl.ds(32 * u, 32)]


def turn(rows):
    return pl.pallas_call(
        turn_kernel,
        out_shape=(jax.ShapeDtypeStruct((128, WIDTH), BF16),) * 2,
        in_specs=[vm()] * 4,
        out_specs=(vm(),) * 2,
        compiler_params=params(),
        cost_estimate=pl.CostEstimate(flops=0, bytes_accessed=2**20, transcendentals=0),
    )(*rows)


def margin_kernel(mine, other, back_own, back_in, target, out):
    total = mine[:ROWS] + other[ROWS:]
    denom = total[:, 0:1]
    stat = total[:, 64:65] / denom
    margin = stat - 0.5 * (stat + (back_own[:, 0:1] + back_in[:, 0:1]) / denom)
    row = jnp.transpose(jnp.broadcast_to(margin, (ROWS, 128)))
    both = jnp.concatenate([row[0:1], target[...]], axis=0)
    for d in range(16):
        out[d] = both


def margins(mine, other, back_own, back_in, target):
    return pl.pallas_call(
        margin_kernel,
        out_shape=jax.ShapeDtypeStruct((16, 2, ROWS), F32),
        in_specs=[vm()] * 5,
        out_specs=vm(),
        compiler_params=params(),
        cost_estimate=pl.CostEstimate(flops=2**18, bytes_accessed=2**20, transcendentals=0),
    )(mine, other, back_own, back_in, target)


def slots_kernel(labels, out):
    zh, y, zl = lax.axis_index("zh"), lax.axis_index("y"), lax.axis_index("zl")
    slot = slot_row(labels[...], zl)
    bucket = slot >> 6
    peer = ((bucket >> 2) ^ zh) * 8 + (((slot >> 5) & 1) ^ zl) * 4 + ((y - (bucket & 3)) & 3)
    place = peer * 32 + (slot & 31)
    out[...] = jnp.transpose((lax.broadcasted_iota(I32, (PACK, ROWS), 0) == place).astype(F32)).astype(BF16)


def slots(labels):
    return pl.pallas_call(
        slots_kernel,
        out_shape=jax.ShapeDtypeStruct((ROWS, PACK), BF16),
        in_specs=[vm()],
        out_specs=vm(),
        compiler_params=params(),
        cost_estimate=pl.CostEstimate(flops=2**24, bytes_accessed=2**19, transcendentals=0),
    )(labels)


def unpack_kernel(place, g0, g1, g2, g3, partner, token):
    got = jnp.concatenate([g[...] for g in (g0, g1, g2, g3)], axis=0)
    partner[...] = jnp.dot(place[...], got, preferred_element_type=F32)
    token[...] = jnp.zeros_like(token)


def unpack(place, got):
    return pl.pallas_call(
        unpack_kernel,
        out_shape=(jax.ShapeDtypeStruct((ROWS, WIDTH), F32), jax.ShapeDtypeStruct((8, 128), F32)),
        in_specs=[vm()] * 5,
        out_specs=(vm(), vm()),
        compiler_params=params(),
        cost_estimate=pl.CostEstimate(flops=2 * PACK * ROWS * WIDTH, bytes_accessed=2**21, transcendentals=0),
    )(place, *got)


def finish_kernel(src_labels, tgt_labels, got, after, src_out, tgt_out):
    del after
    for kind, labels, out in ((0, src_labels, src_out), (1, tgt_labels, tgt_out)):
        slot = slot_row(labels[...], lax.axis_index("zl"))
        column = lax.axis_index(("zh", "y")) * 32 + (slot & 31)
        place = (lax.broadcasted_iota(I32, (ROWS, ROWS), 0) == column).astype(BF16)
        values = jnp.concatenate([got[s, kind : kind + 1] for s in range(16)], axis=0)
        found = jnp.zeros((16, ROWS), F32)
        for _ in range(3):
            piece = values.astype(BF16)
            values = values - piece.astype(F32)
            found = found + jnp.dot(piece, place, preferred_element_type=F32)
        here = lax.broadcasted_iota(I32, (16, ROWS), 0) == (slot >> 5)
        out[...] = jnp.sum(jnp.where(here, found, 0.0), axis=0, keepdims=True)


def finish(src_labels, tgt_labels, got, after):
    return pl.pallas_call(
        finish_kernel,
        out_shape=(jax.ShapeDtypeStruct((1, ROWS), F32),) * 2,
        in_specs=[vm()] * 3 + [hbm()],
        out_specs=(vm(), vm()),
        compiler_params=params(),
        cost_estimate=pl.CostEstimate(flops=2**24, bytes_accessed=2**16, transcendentals=0),
    )(src_labels, tgt_labels, got, after)


def route(packed):
    return lax.all_to_all(packed, ROUTE, 0, 0, tiled=True)


def shift(d):
    return [(i, (i + d) % 4) for i in range(4)]


def on_device(source, source_label, target, target_label):
    src_labels, tgt_labels = source_label.reshape(1, ROWS), target_label.reshape(1, ROWS)
    place = slots(src_labels)

    base = merge(route(pack(tgt_labels, target)))
    left, right = lax.ppermute(base, "x", RIGHT), lax.ppermute(base, "x", LEFT)
    across = lax.ppermute(base, "zl", SWAP)
    go_right, go_left = regroup((left, right), (((0, 0),), ((1, 1),)))
    far_first, far_second = lax.ppermute(go_right, "x", RIGHT), lax.ppermute(go_left, "x", LEFT)
    across_left, across_right = lax.ppermute(across, "x", RIGHT), lax.ppermute(across, "x", LEFT)
    (far,) = regroup((far_first, far_second), (((0, 0), (1, 0)),))
    last = lax.ppermute(far, "zl", SWAP)

    src_own = merge(route(pack(src_labels, source, base)), far_first, far_second)
    src_sib = lax.ppermute(src_own, "c", SWAP)
    calls = (
        (
            (base, left, right, across, far),
            ((0, 0), (0, 1), (1, 0), (1, 1), (2, 0), (2, 1), (3, 0), (3, 1), (4, 0), (4, 1)),
        ),
        (
            (last, across_left, across_right),
            ((0, 0), (0, 1), (1, 0), (1, 1), (2, 0), (2, 1)),
        ),
    )
    parts, carry = [], ()
    for n, (arrays, pieces) in enumerate(calls):
        weight, tot, wsum, own, sib, *fwd = score(src_own, src_sib, arrays, pieces, carry, n == 1)
        parts.append((weight, tot, wsum))
        carry = (*fwd, own, sib)
    (fwd,) = fwd
    fwd_in = lax.ppermute(fwd, "c", SWAP)
    partner_in = lax.ppermute(sib, "c", SWAP)

    by_y = home(fwd, fwd_in, own, partner_in)
    by_y = (by_y[0],) + tuple(lax.ppermute(by_y[d], "y", shift(d)) for d in (1, 2, 3))
    same, flip = turn(by_y)
    got = [same] + [
        lax.ppermute(rows, ("zh", "zl"), [(i, i ^ z) for i in range(4)]) for z, rows in ((1, same), (2, flip), (3, flip))
    ]
    partner_out, token = unpack(place, got)

    heard = lax.all_to_all(fore(fwd, fwd_in, by_y[0], parts), PLANE, 0, 0, tiled=True)
    back_own, back_sib, tgt_margin = back(heard, parts[0][0], parts[1][0])
    back_in = lax.ppermute(back_sib, "c", SWAP)
    both = route(margins(fwd, fwd_in, back_own, back_in, tgt_margin))
    src_margin, tgt_margin = finish(src_labels, tgt_labels, both, token)
    return (partner_out, src_margin.reshape(ROWS), tgt_margin.reshape(ROWS))


def solution(mesh):
    fine = Mesh(mesh.devices.reshape(2, 4, 2, 4, 2), AXES)
    return jax.shard_map(
        on_device,
        mesh=fine,
        in_specs=(P(AXES, None), P(AXES), P(AXES, None), P(AXES)),
        out_specs=(P(AXES, None), P(AXES), P(AXES)),
        check_vma=False,
    )
```
